128 devices in a mesh: gx: 16 (over x, y), gy: 8 (over z, core).
Axes of the slice: x: 4, y: 4, z: 4, core: 2. Of those that a mesh axis runs over, the one named last changes fastest.
Arguments:
- theta: float32 [10, 128, 128, 128], P(None, 'gx', 'gy'), may hold values from -6 to 6
- phi_table: float32 [1024, 100], replicated, may hold values from -0.1 to 0.3
- dphi_table: float32 [1024, 100], replicated, may hold values from -0.5 to 1
Outputs:
- u_grids: float32 [10, 128, 128, 128], P(None, 'gx', 'gy')
- stress: float32 [3, 3], replicated
- energy: float32 [], replicated
The draws below stay inside these ranges and needn't reach their ends.
All inputs are finite; a program needn't handle non-finite values.
Results may differ from the reference program's by a relative error of at most 0.0003.
Values sent between devices are 32-bit elements; how exact they have to be, the bound alone decides.
A program may use at most 64 MiB of HBM per device.

```python
import math
import jax
import jax.numpy as jnp
from jax import lax

NX = 128
NY = 128
NZ = 128
Q = 10
NK = 1024
QQ = 100


def steps_of(own_key, extent, shards, smallest, top_value):
    factor_of, own = 1.0, jax.random.fold_in(own_key, 6)
    for dim, parts in shards:
        heights = jnp.exp(jax.random.uniform(jax.random.fold_in(own, dim), (parts,), jnp.float32, smallest / len(shards), top_value / len(shards)))
        factor_of = factor_of * jnp.repeat(heights, extent[dim] // parts).reshape([-1 if axis == dim else 1 for axis in range(len(extent))])
    return factor_of


def normal_values(key, dims, spread, bound, pieces=(), kind=jnp.bfloat16):
    gain = steps_of(key, dims, pieces, -0.22, 0.18) if pieces else 1.0
    result = jax.random.normal(key, dims, jnp.float32) * spread * gain
    return jnp.minimum(jnp.maximum(result, -bound), bound).astype(kind)


def setup_inputs(seed: int = 0) -> dict:
    keys = jax.random.split(jax.random.key(seed), 4)
    return {
        "theta": normal_values(keys[0], (Q, NX, NY, NZ), 1.0, 6.0, ((1, 16), (2, 8)), jnp.float32),
        "phi_table": jnp.clip(jax.random.uniform(keys[1], (NK, QQ), jnp.float32, -0.1, 0.3), -0.1, 0.3),
        "dphi_table": jnp.clip(jax.random.uniform(keys[2], (NK, QQ), jnp.float32, -0.5, 1.0), -0.5, 1.0),
    }


HIGHEST = lax.Precision.HIGHEST

def wave_numbers(length):
    position = jnp.arange(length, dtype=jnp.int32)
    shifted = (position + length // 2) % length - length // 2
    return shifted.astype(jnp.float32) * (2.0 * math.pi / length)

def reference(theta, phi_table, dphi_table):
    spectrum = jnp.fft.fftn(theta, axes=(1, 2, 3))
    spec_real = jnp.real(spectrum)
    spec_imag = jnp.imag(spectrum)
    wave_x = wave_numbers(NX)
    wave_y = wave_numbers(NY)
    wave_z = wave_numbers(NZ)
    radial_scale = (NK - 1) / (math.pi * math.sqrt(3.0))
    grid_y = jnp.broadcast_to(wave_y[:, None], (NY, NZ))
    grid_z = jnp.broadcast_to(wave_z[None, :], (NY, NZ))

    def one_plane(plane_index):
        part_real = lax.dynamic_index_in_dim(spec_real, plane_index, 1, keepdims=False)
        part_imag = lax.dynamic_index_in_dim(spec_imag, plane_index, 1, keepdims=False)
        along_x = lax.dynamic_index_in_dim(wave_x, plane_index, 0, keepdims=False)
        radial = jnp.sqrt(along_x * along_x + grid_y * grid_y + grid_z * grid_z) * radial_scale
        lower_point = jnp.clip(jnp.floor(radial), 0.0, NK - 2.0)
        fraction = (radial - lower_point)[:, :, None]
        lower_index = lower_point.astype(jnp.int32)
        kernel = (1.0 - fraction) * phi_table[lower_index] + fraction * phi_table[lower_index + 1]
        kernel_slope = (1.0 - fraction) * dphi_table[lower_index] + fraction * dphi_table[lower_index + 1]
        kernel = kernel.reshape(NY, NZ, Q, Q)
        kernel_slope = kernel_slope.reshape(NY, NZ, Q, Q)
        u_real = jnp.einsum('yzqp,pyz->qyz', kernel, part_real, precision=HIGHEST)
        u_imag = jnp.einsum('yzqp,pyz->qyz', kernel, part_imag, precision=HIGHEST)
        grad_real = jnp.einsum('yzqp,pyz->qyz', kernel_slope, part_real, precision=HIGHEST)
        grad_imag = jnp.einsum('yzqp,pyz->qyz', kernel_slope, part_imag, precision=HIGHEST)
        weight = lax.optimization_barrier(jnp.sum(part_real * grad_real + part_imag * grad_imag, axis=0))
        moments = jnp.stack([jnp.sum(weight * along_x * along_x), jnp.sum(weight * grid_y * grid_y), jnp.sum(weight * grid_z * grid_z), jnp.sum(weight * along_x * grid_y), jnp.sum(weight * along_x * grid_z), jnp.sum(weight * grid_y * grid_z)])
        return (u_real, u_imag, moments)
    u_real, u_imag, moments = lax.map(one_plane, jnp.arange(NX, dtype=jnp.int32))
    u_spec = jnp.transpose(u_real + 1j * u_imag, (1, 0, 2, 3))
    u_grids = jnp.real(jnp.fft.ifftn(u_spec, axes=(1, 2, 3))).astype(jnp.float32)
    cell_total = NX * NY * NZ
    energy = jnp.sum(theta * u_grids) * (0.5 / cell_total)
    stress_terms = lax.optimization_barrier(jnp.sum(moments, axis=0)) * (-0.5 / (cell_total * cell_total))
    stress = jnp.stack([jnp.stack([stress_terms[0], stress_terms[3], stress_terms[4]]), jnp.stack([stress_terms[3], stress_terms[1], stress_terms[5]]), jnp.stack([stress_terms[4], stress_terms[5], stress_terms[2]])])
    return (u_grids, stress, energy)
```

```python
import functools
import math

import jax
import jax.numpy as jnp
import ml_dtypes
import numpy as np
from jax import lax
from jax.experimental import pallas as pl
from jax.experimental.pallas import tpu as pltpu
from jax.sharding import PartitionSpec as P

MESH = pl.DeviceIdType.MESH
F32 = jnp.float32
BF16 = jnp.bfloat16
N = 128
HALF = 64
Q = 10
GX = 16
GY = 8
NC = 5
NQ = Q // NC
PAIRS = 160
KROWS = 72
TABLE = 1024


def real_basis():
    r = np.arange(N)
    rows = [np.full(N, 1.0) / np.sqrt(N)]
    rows += [np.cos(2 * np.pi * k * r / N) * np.sqrt(2.0 / N) for k in range(1, HALF)]
    rows += [np.cos(np.pi * r) / np.sqrt(N)]
    rows += [np.sin(2 * np.pi * k * r / N) * np.sqrt(2.0 / N) for k in range(1, HALF)]
    return np.array(rows)


def halves(array):
    high = array.astype(ml_dtypes.bfloat16)
    low = (array - high.astype(np.float64)).astype(ml_dtypes.bfloat16)
    return np.stack([high, low])


def sym_index(q, p):
    q, p = min(q, p), max(q, p)
    return 100 + q * Q - q * (q - 1) // 2 + (p - q)


def constants():
    basis = real_basis()
    order = np.array([(lane // 2) + HALF * (lane % 2) for lane in range(N)])
    z_basis = basis[order]
    pick = np.zeros((2, PAIRS, Q * Q))
    for pair in range(Q * Q):
        pick[0, pair, pair] = 1.0
    for q in range(Q):
        for p in range(q, Q):
            pick[1, sym_index(q, p), q * Q + p] += 0.5
            pick[1, sym_index(q, p), p * Q + q] += 0.5
    return (
        halves(z_basis.T),
        halves(z_basis),
        halves(basis),
        halves(basis.T),
        pick.astype(ml_dtypes.bfloat16),
    )


def split(value):
    high = value.astype(BF16)
    return high, (value - high.astype(F32)).astype(BF16)


def mm(a, b, dims=(((1,), (0,)), ((), ()))):
    return lax.dot_general(a, b, dims, preferred_element_type=F32)


def mm3(a, b, dims=(((1,), (0,)), ((), ()))):
    (ah, al), (bh, bl) = a, b
    return mm(ah, bh, dims) + (mm(al, bh, dims) + mm(ah, bl, dims))


def lanes_iota(rows):
    return lax.broadcasted_iota(jnp.int32, (rows, N), 1)


def turn(values, back):
    values = list(values)
    lane = lax.broadcasted_iota(jnp.int32, values[0].shape, values[0].ndim - 1)
    axis = values[0].ndim - 1
    for bit in (0, 1, 2):
        step = 1 << bit
        low = (lane & step) == 0
        for i in range(8):
            if i & step:
                continue
            j = i | step
            first, second = values[i], values[j]
            values[i] = jnp.where(low, first, pltpu.roll(second, step, axis))
            values[j] = jnp.where(low, pltpu.roll(first, N - step, axis), second)
    return values


def kernel(theta, phi, dphi, zf, zb, xf, xb, pick, u_out, stress_out, energy_out,
           s1, b1, p1, a1, spec, uspec, grad, v1, a2, w1, c1, partner, ktab, tabs, sums_a, sums_b, part,
           send_sem, recv1, recv2, recv3, recv4, sib_sem, sum_sem):
    gx = lax.axis_index("gx")
    gy = lax.axis_index("gy")
    core = lax.rem(gy, 2)
    plane = gx * GY + gy
    kz_low = plane // 2
    is_znyq = plane == 1
    kz = jnp.where(is_znyq, HALF, kz_low)
    sib = gy + 1 - 2 * core

    barrier = pltpu.get_barrier_semaphore()

    def hello_y(i, c):
        pl.semaphore_signal(barrier, inc=1, device_id=(gx, lax.rem(gy + i, GY)), device_id_type=MESH)
        return c

    def hello_x(i, c):
        pl.semaphore_signal(barrier, inc=1, device_id=(lax.rem(gx + i, GX), gy), device_id_type=MESH)
        return c

    lax.fori_loop(1, GY, hello_y, 0)
    lax.fori_loop(1, GX, hello_x, 0)

    zfh, zfl = zf[0], zf[1]
    for c in range(NC):
        block = theta[pl.ds(c * NQ, NQ)].reshape(NQ * 8 * 16, N)
        out = mm3(split(block), (zfh, zfl)).reshape(NQ, 8, 16, N)
        turned = turn([out[:, x] for x in range(8)], False)
        for g in range(GY):
            s1[g, pl.ds(c * NQ, NQ)] = turned[g]

    pl.semaphore_wait(barrier, GX + GY - 2)

    for c in range(NC):
        qs = pl.ds(c * NQ, NQ)

        def send1(i, k, qs=qs, c=c):
            to = lax.rem(gy + i, GY)
            pltpu.make_async_remote_copy(
                s1.at[to, qs], b1.at[qs, pl.ds(gy * 16, 16)], send_sem.at[0], recv1.at[c],
                device_id=(gx, to), device_id_type=MESH).start()
            return k

        lax.fori_loop(1, GY, send1, 0)
        b1[qs, pl.ds(gy * 16, 16)] = s1[gy, qs]

    phi_h, phi_l = split(phi[...])
    dphi_h, dphi_l = split(dphi[...])
    nt = (((1,), (1,)), ((), ()))
    table = (mm(pick[0], phi_h, nt) + mm(pick[0], phi_l, nt)) + (mm(pick[1], dphi_h, nt) + mm(pick[1], dphi_l, nt))
    tabs[0:PAIRS], tabs[PAIRS:2 * PAIRS] = split(table)
    tabs[2 * PAIRS:3 * PAIRS], tabs[3 * PAIRS:] = split(pltpu.roll(table, TABLE - 1, 1) - table)

    lane256 = lax.broadcasted_iota(jnp.int32, (1, 2 * N), 1)
    ky256 = jnp.where(lax.rem(lane256, N) == HALF, HALF, lane256 & (HALF - 1))
    second256 = lane256 // N

    def look_up(step, width):
        row = 2 * step
        first = jnp.where(row > HALF, row - HALF, row)
        near = first * first + kz * kz
        start = 0
        if width < TABLE:
            for t in range(1, (TABLE - width) // N + 1):
                start = start + jnp.minimum(near // math.ceil(t * t * 128.0 * 128.0 * 3 * 4096 / (1023.0 * 1023.0)), 1)
        base = pl.multiple_of(start * N, N)
        kx = row + second256
        kx = jnp.where(kx > HALF, kx - HALF, kx)
        square = kx * kx + ky256 * ky256 + kz * kz
        radial = jnp.sqrt(square.astype(F32)) * ((TABLE - 1) / (HALF * math.sqrt(3.0)))
        lower = jnp.clip(jnp.floor(radial), 0.0, TABLE - 2.0)
        fraction = radial - lower
        index = lower.astype(jnp.int32) - start * N
        points = lax.broadcasted_iota(jnp.int32, (width, 2 * N), 0)
        onehot = jnp.where(points == index, 1.0, 0.0).astype(BF16)
        out = mm(tabs[:, pl.ds(base, width)], onehot)
        value = (out[0:PAIRS] + out[PAIRS:2 * PAIRS]) + fraction * (out[2 * PAIRS:3 * PAIRS] + out[3 * PAIRS:])
        ktab[pl.ds(row, PAIRS, stride=KROWS), :] = value[:, 0:N]
        ktab[pl.ds(row + 1, PAIRS, stride=KROWS), :] = value[:, N:]

    def look_wide(step, k):
        look_up(step, TABLE)
        return k

    def look_narrow(step, k):
        look_up(step, 512)
        return k

    lax.fori_loop(0, 15, look_wide, 0)

    xfh, xfl = xf[0], xf[1]
    xbh, xbl = xb[0], xb[1]
    for c in range(NC):
        qs = pl.ds(c * NQ, NQ)
        got = b1.at[qs, pl.ds(0, 112)]
        pltpu.make_async_copy(got, got, recv1.at[c]).wait()
        for q in range(c * NQ, (c + 1) * NQ):
            p1[q] = mm3(split(b1[q].T), (xbh, xbl))

        def send2(i, k, qs=qs, c=c):
            to = lax.rem(gx + i, GX)
            pltpu.make_async_remote_copy(
                p1.at[qs, pl.ds(to * 8, 8)], a1.at[qs, pl.ds(gx * 8, 8)], send_sem.at[1], recv2.at[c],
                device_id=(to, gy), device_id_type=MESH).start()
            return k

        lax.fori_loop(1, GX, send2, 0)
        a1[qs, pl.ds(gx * 8, 8)] = p1[qs, pl.ds(gx * 8, 8)]
        first = 15 + 4 * c
        if c < NC - 1:
            lax.fori_loop(first, first + 4, look_narrow, 0)
        else:
            lax.fori_loop(first, 32, look_narrow, 0)
            lax.fori_loop(32, 36, look_wide, 0)

    for c in range(NC):
        qs = pl.ds(c * NQ, NQ)
        got = a1.at[qs, pl.ds(0, 120)]
        pltpu.make_async_copy(got, got, recv2.at[c]).wait()
        for q in range(c * NQ, (c + 1) * NQ):
            spec[q] = mm3((xfh, xfl), split(a1[q])).reshape(2, HALF, N)

    to_sibling = pltpu.make_async_remote_copy(
        spec.at[:, :, pl.ds((1 - core) * 32, 32)], partner, sib_sem.at[0], sib_sem.at[1],
        device_id=(gx, sib), device_id_type=MESH)
    to_sibling.start()

    def contract(tile, energy):
        parity = tile // 8
        place = pl.ds(pl.multiple_of(lax.rem(tile, 8) * 8, 8), 8)
        krow = jnp.where(tile == 8, HALF, lax.rem(tile, 8) * 8)
        s = [spec[q, parity, place] for q in range(Q)]
        for q in range(Q):
            acc = None
            for p in range(Q):
                term = ktab[pl.ds(pl.multiple_of((q * Q + p) * KROWS + krow, 8), 8), :] * s[p]
                acc = term if acc is None else acc + term
            uspec[q, parity, place] = acc
            energy = energy + acc * s[q]
        return energy

    zero = jnp.zeros((8, N), F32)
    energy = lax.fori_loop(0, 16, contract, zero)

    for c in range(NC):
        qs = pl.ds(c * NQ, NQ)
        for q in range(c * NQ, (c + 1) * NQ):
            v1[q] = mm3((xbh, xbl), split(uspec[q].reshape(N, N)))

        def send3(i, k, qs=qs, c=c):
            to = lax.rem(gx + i, GX)
            pltpu.make_async_remote_copy(
                v1.at[qs, pl.ds(to * 8, 8)], a2.at[qs, pl.ds(gx * 8, 8)], send_sem.at[2], recv3.at[c],
                device_id=(to, gy), device_id_type=MESH).start()
            return k

        lax.fori_loop(1, GX, send3, 0)
        a2[qs, pl.ds(gx * 8, 8)] = v1[qs, pl.ds(gx * 8, 8)]

    lane = lanes_iota(8)
    sub = lax.broadcasted_iota(jnp.int32, (8, N), 0)
    j = lane & (HALF - 1)
    ky_off = j.astype(F32)
    ky_full = jnp.where(lane == HALF, HALF, j).astype(F32)
    sy = lane // HALF
    ynyq = lane == HALF
    top = float(HALF * HALF)
    kz_f = kz.astype(F32)
    kz_off = kz_low.astype(F32)

    def moments(tile, sums):
        parity = tile // 8
        place = pl.ds(pl.multiple_of(lax.rem(tile, 8) * 8, 8), 8)
        krow = jnp.where(tile == 8, HALF, lax.rem(tile, 8) * 8)
        s = [spec[q, parity, place] for q in range(Q)]
        weight = zero
        cross = zero
        for q in range(Q):
            acc = None
            for p in range(Q):
                term = ktab[pl.ds(pl.multiple_of(sym_index(q, p) * KROWS + krow, 8), 8), :] * s[p]
                acc = term if acc is None else acc + term
            grad[q, parity, place] = acc
            weight = weight + acc * s[q]
            cross = cross + acc * pltpu.roll(spec[q, 1 - parity, place], HALF, 1)
        i = lax.rem(tile, 8) * 8 + sub
        kx_off = i.astype(F32)
        xnyq = (i == 0) & (parity == 1)
        kx_full = jnp.where(xnyq, top, kx_off * kx_off)
        xx, yy, zz, xy, xz, yz = sums
        xx = xx + weight * kx_full
        yy = yy + weight * (ky_full * ky_full)
        zz = zz + weight
        sign = jnp.where(sy == parity, -1.0, 1.0)
        xy = xy + cross * (sign * kx_off * ky_off) + jnp.where(xnyq & ynyq, weight * top, 0.0)
        xz = xz + jnp.where(xnyq & is_znyq, weight * top, 0.0)
        yz = yz + jnp.where(ynyq & is_znyq, weight * top, 0.0)
        return xx, yy, zz, xy, xz, yz

    xx, yy, zz, xy, xz, yz = lax.fori_loop(0, 16, moments, (zero,) * 6)

    to_sibling.wait()

    def mixed(step, sums):
        parity = step // 4
        here = lax.rem(step, 4) * 8
        mine = pl.ds(pl.multiple_of(core * 32 + here, 8), 8)
        theirs = pl.ds(pl.multiple_of(here, 8), 8)
        along_x = zero
        along_y = zero
        for q in range(Q):
            g = grad[q, parity, mine]
            along_x = along_x + g * partner[q, 1 - parity, theirs]
            along_y = along_y + g * pltpu.roll(partner[q, parity, theirs], HALF, 1)
        kx_off = (core * 32 + here + sub).astype(F32)
        xz, yz = sums
        xz = xz + along_x * (jnp.where(parity == core, -2.0, 2.0) * kz_off * kx_off)
        yz = yz + along_y * (jnp.where(sy == core, -2.0, 2.0) * kz_off * ky_off)
        return xz, yz

    xz, yz = lax.fori_loop(0, 8, mixed, (xz, yz))
    zz = zz * (kz_f * kz_f)
    part[...] = zero
    for row, total in enumerate((energy, xx, yy, zz, xy, xz, yz)):
        part[pl.ds(row, 1)] = jnp.sum(total, axis=0, keepdims=True)
    sums_a[gy] = part[...]

    def send_sum_y(i, k):
        to = lax.rem(gy + i, GY)
        pltpu.make_async_remote_copy(part, sums_a.at[gy], send_sem.at[4], sum_sem.at[0],
                                     device_id=(gx, to), device_id_type=MESH).start()
        return k

    lax.fori_loop(1, GY, send_sum_y, 0)

    for c in range(NC):
        qs = pl.ds(c * NQ, NQ)
        got = a2.at[qs, pl.ds(0, 120)]
        pltpu.make_async_copy(got, got, recv3.at[c]).wait()
        for q in range(c * NQ, (c + 1) * NQ):
            w1[q] = mm3((xbh, xbl), split(a2[q].T))

        def send4(i, k, qs=qs, c=c):
            to = lax.rem(gy + i, GY)
            pltpu.make_async_remote_copy(
                w1.at[qs, pl.ds(to * 16, 16)], c1.at[gy, qs], send_sem.at[3], recv4.at[c],
                device_id=(gx, to), device_id_type=MESH).start()
            return k

        lax.fori_loop(1, GY, send4, 0)
        c1[gy, qs] = w1[qs, pl.ds(gy * 16, 16)]

    got = sums_a.at[pl.ds(0, GY - 1)]
    pltpu.make_async_copy(got, got, sum_sem.at[0]).wait()
    total = sums_a[0]
    for i in range(1, GY):
        total = total + sums_a[i]
    sums_b[gx] = total

    def send_sum_x(i, k):
        to = lax.rem(gx + i, GX)
        pltpu.make_async_remote_copy(sums_b.at[gx], sums_b.at[gx], send_sem.at[5], sum_sem.at[1],
                                     device_id=(to, gy), device_id_type=MESH).start()
        return k

    lax.fori_loop(1, GX, send_sum_x, 0)

    zbh, zbl = zb[0], zb[1]
    for c in range(NC):
        qs = pl.ds(c * NQ, NQ)
        got = c1.at[pl.ds(0, GY - 1), qs]
        pltpu.make_async_copy(got, got, recv4.at[c]).wait()
        turned = turn([c1[g, qs] for g in range(GY)], True)
        for x in range(8):
            block = mm3(split(turned[x].reshape(NQ * 16, N)), (zbh, zbl))
            u_out[qs, x] = block.reshape(NQ, 16, N)

    got = sums_b.at[pl.ds(0, GX - 1)]
    pltpu.make_async_copy(got, got, sum_sem.at[1]).wait()
    total = sums_b[0]
    for i in range(1, GX):
        total = total + sums_b[i]
    cells = float(N) ** 3
    wave = (2.0 * math.pi / N) ** 2
    sums = jnp.sum(total, axis=1, keepdims=True)
    row = lax.broadcasted_iota(jnp.int32, (8, 1), 0)

    def pick_sum(r):
        return jnp.sum(jnp.where(row == r, sums, 0.0), axis=0, keepdims=True)

    energy_out[...] = pick_sum(0) * (0.5 / cells)
    r3 = lax.broadcasted_iota(jnp.int32, (3, 3), 0)
    c3 = lax.broadcasted_iota(jnp.int32, (3, 3), 1)
    stress = jnp.zeros((3, 3), F32)
    for r, (a, b) in enumerate(((0, 0), (1, 1), (2, 2), (0, 1), (0, 2), (1, 2))):
        here = ((r3 == a) & (c3 == b)) | ((r3 == b) & (c3 == a))
        stress = jnp.where(here, pick_sum(r + 1) * (-0.5 * wave / cells), stress)
    stress_out[...] = stress

    for slot, buffer in ((0, s1.at[pl.ds(0, GY - 1)]), (1, p1.at[:, pl.ds(0, 120)]), (2, v1.at[:, pl.ds(0, 120)]),
                         (3, w1.at[:, pl.ds(0, 112)]), (4, sums_a.at[pl.ds(0, GY - 1)]), (5, sums_b.at[pl.ds(0, GX - 1)])):
        pltpu.make_async_copy(buffer, buffer, send_sem.at[slot]).wait()


def shards(theta, phi, dphi):
    vmem = pl.BlockSpec(memory_space=pltpu.VMEM)
    cube = pltpu.VMEM((Q, N, N), F32)
    halves_cube = pltpu.VMEM((Q, 2, HALF, N), F32)
    small = pltpu.VMEM((GY, Q, 16, N), F32)
    u, stress, energy = pl.pallas_call(
        kernel,
        out_shape=(
            jax.ShapeDtypeStruct((Q, 8, 16, N), F32),
            jax.ShapeDtypeStruct((3, 3), F32),
            jax.ShapeDtypeStruct((1, 1), F32),
        ),
        in_specs=[vmem] * 8,
        out_specs=(vmem,) * 3,
        scratch_shapes=[
            small, cube, cube, cube, halves_cube, halves_cube, halves_cube, cube, cube, cube, small,
            pltpu.VMEM((Q, 2, 32, N), F32),
            pltpu.VMEM((PAIRS * KROWS, N), F32),
            pltpu.VMEM((4 * PAIRS, TABLE), BF16),
            pltpu.VMEM((GY, 8, N), F32),
            pltpu.VMEM((GX, 8, N), F32),
            pltpu.VMEM((8, N), F32),
            pltpu.SemaphoreType.DMA((6,)),
            pltpu.SemaphoreType.DMA((NC,)),
            pltpu.SemaphoreType.DMA((NC,)),
            pltpu.SemaphoreType.DMA((NC,)),
            pltpu.SemaphoreType.DMA((NC,)),
            pltpu.SemaphoreType.DMA((2,)),
            pltpu.SemaphoreType.DMA((2,)),
        ],
        compiler_params=pltpu.CompilerParams(
            collective_id=0, has_side_effects=True, vmem_limit_bytes=48 << 20),
    )(theta, phi, dphi, *(jnp.asarray(c) for c in constants()))
    return u, stress, energy.reshape(())


def solution(mesh):
    return jax.shard_map(
        shards,
        mesh=mesh,
        in_specs=(P(None, "gx", "gy", None), P(), P()),
        out_specs=(P(None, "gx", "gy", None), P(), P()),
        check_vma=False,
    )
```

```python
import functools
import math

import jax
import jax.numpy as jnp
import ml_dtypes
import numpy as np
from jax import lax
from jax.experimental import pallas as pl
from jax.experimental.pallas import tpu as pltpu
from jax.sharding import PartitionSpec as P

MESH = pl.DeviceIdType.MESH
F32 = jnp.float32
BF16 = jnp.bfloat16
N = 128
HALF = 64
Q = 10
GX = 16
EARLY = 10
FIRST = 64
GY = 8
ROWS = 10
PAIRS = 160
KROWS = 72
TABLE = 1024


def real_basis():
    r = np.arange(N)
    rows = [np.full(N, 1.0) / np.sqrt(N)]
    rows += [np.cos(2 * np.pi * k * r / N) * np.sqrt(2.0 / N) for k in range(1, HALF)]
    rows += [np.cos(np.pi * r) / np.sqrt(N)]
    rows += [np.sin(2 * np.pi * k * r / N) * np.sqrt(2.0 / N) for k in range(1, HALF)]
    return np.array(rows)


def halves(array):
    high = array.astype(ml_dtypes.bfloat16)
    low = (array - high.astype(np.float64)).astype(ml_dtypes.bfloat16)
    return np.stack([high, low])


def sym_index(q, p):
    q, p = min(q, p), max(q, p)
    return 100 + q * Q - q * (q - 1) // 2 + (p - q)


def constants():
    basis = real_basis()
    order = np.array([(lane // 2) + HALF * (lane % 2) for lane in range(N)])
    z_basis = basis[order]
    by_source = np.array([(i % GX) * 8 + i // GX for i in range(N)])
    x_basis = basis[:, by_source]
    pick = np.zeros((2, PAIRS, Q * Q))
    for pair in range(Q * Q):
        pick[0, pair, pair] = 1.0
    for q in range(Q):
        for p in range(q, Q):
            pick[1, sym_index(q, p), q * Q + p] += 0.5
            pick[1, sym_index(q, p), p * Q + q] += 0.5
    bases = np.stack([halves(b) for b in (z_basis, x_basis, x_basis.T, basis, basis.T)])
    return bases, pick.astype(ml_dtypes.bfloat16)


def split(value):
    high = value.astype(BF16)
    return high, (value - high.astype(F32)).astype(BF16)


def mm(a, b, dims=(((1,), (0,)), ((), ()))):
    return lax.dot_general(a, b, dims, preferred_element_type=F32)


def mm3(a, b, dims=(((1,), (0,)), ((), ()))):
    (ah, al), (bh, bl) = a, b
    return mm(ah, bh, dims) + (mm(al, bh, dims) + mm(ah, bl, dims))


def lanes_iota(rows):
    return lax.broadcasted_iota(jnp.int32, (rows, N), 1)


def exchange(values, lane_step):
    values = list(values)
    axis = values[0].ndim - 1
    lane = lax.broadcasted_iota(jnp.int32, values[0].shape, axis)
    bit = 1
    while bit < len(values):
        step = bit * lane_step
        low = (lane & step) == 0
        for i in range(len(values)):
            if i & bit:
                continue
            first, second = values[i], values[i | bit]
            values[i] = jnp.where(low, first, pltpu.roll(second, step, axis))
            values[i | bit] = jnp.where(low, pltpu.roll(first, N - step, axis), second)
        bit *= 2
    return values


def kernel(theta_in, phi_in, dphi_in, bases_in, pick_in, u_out, stress_out, energy_out,
           theta, phi, dphi, bases, pick, s1, r1, s2, r2, mid, spec, uspec, grad, partner, ktab, tabs, sums_a, sums_b, part,
           send_sem, recv_sem, own_sem, sib_sem, sum_sem, in_sem):
    inputs = [pltpu.make_async_copy(source, target, in_sem.at[i]) for i, (source, target) in enumerate(
        ((theta_in, theta), (bases_in, bases), (phi_in, phi), (dphi_in, dphi), (pick_in, pick)))]
    for copy in inputs:
        copy.start()
    gx = lax.axis_index("gx")
    gy = lax.axis_index("gy")
    core = lax.rem(gy, 2)
    plane = gx * GY + gy
    place_in_order = gy * GX + gx
    kz_low = plane // 2
    is_znyq = plane == 1
    kz = jnp.where(is_znyq, HALF, kz_low)
    sib = gy + 1 - 2 * core

    barrier = pltpu.get_barrier_semaphore()

    def hello(i, c):
        to = lax.rem(plane + i, N)
        pl.semaphore_signal(barrier, inc=1, device_id=(to // GY, lax.rem(to, GY)), device_id_type=MESH)
        return c

    lax.fori_loop(1, N, hello, 0)

    nt = (((1,), (1,)), ((), ()))
    inputs[0].wait()
    inputs[1].wait()
    zbh, zbl = bases[0, 0], bases[0, 1]
    for x in range(8):
        block = theta[0:8, x].reshape(N, N)
        s1[pl.ds(x, N, stride=ROWS), :] = mm3((zbh, zbl), split(block), nt)
    for r in range(2):
        block = jnp.concatenate([theta[8 + q, 2 * b + r] for b in range(4) for q in range(2)], axis=0)
        s1[pl.ds(8 + r, N, stride=ROWS), :] = mm3((zbh, zbl), split(block), nt)

    for copy in inputs[2:]:
        copy.wait()
    phi_h, phi_l = split(phi[...])
    dphi_h, dphi_l = split(dphi[...])
    table = (mm(pick[0], phi_h) + mm(pick[0], phi_l)) + (mm(pick[1], dphi_h) + mm(pick[1], dphi_l))
    tabs[0:PAIRS], tabs[PAIRS:2 * PAIRS] = split(table)
    tabs[2 * PAIRS:3 * PAIRS], tabs[3 * PAIRS:] = split(pltpu.roll(table, TABLE - 1, 1) - table)

    lane256 = lax.broadcasted_iota(jnp.int32, (1, 2 * N), 1)
    ky256 = jnp.where(lax.rem(lane256, N) == HALF, HALF, lane256 & (HALF - 1))
    second256 = lane256 // N

    def look_up(step, width):
        row = 2 * step
        first = jnp.where(row > HALF, row - HALF, row)
        near = first * first + kz * kz
        start = 0
        if width < TABLE:
            for t in range(1, (TABLE - width) // N + 1):
                start = start + jnp.minimum(near // math.ceil(t * t * 128.0 * 128.0 * 3 * 4096 / (1023.0 * 1023.0)), 1)
        base = pl.multiple_of(start * N, N)
        kx = row + second256
        kx = jnp.where(kx > HALF, kx - HALF, kx)
        square = kx * kx + ky256 * ky256 + kz * kz
        radial = jnp.sqrt(square.astype(F32)) * ((TABLE - 1) / (HALF * math.sqrt(3.0)))
        lower = jnp.clip(jnp.floor(radial), 0.0, TABLE - 2.0)
        fraction = radial - lower
        index = lower.astype(jnp.int32) - start * N
        points = lax.broadcasted_iota(jnp.int32, (width, 2 * N), 0)
        onehot = jnp.where(points == index, 1.0, 0.0).astype(BF16)
        out = mm(tabs[:, pl.ds(base, width)], onehot)
        value = (out[0:PAIRS] + out[PAIRS:2 * PAIRS]) + fraction * (out[2 * PAIRS:3 * PAIRS] + out[3 * PAIRS:])
        ktab[pl.ds(row, PAIRS, stride=KROWS), :] = value[:, 0:N]
        ktab[pl.ds(row + 1, PAIRS, stride=KROWS), :] = value[:, N:]

    def look_wide(step, k):
        look_up(step, 768)
        return k

    def look_narrow(step, k):
        look_up(step, 512)
        return k

    lax.fori_loop(0, EARLY, look_wide, 0)
    pl.semaphore_wait(barrier, N - 1)

    def send1(i, c):
        to = lax.rem(plane + i, N)
        pltpu.make_async_remote_copy(
            s1.at[pl.ds(to * ROWS, ROWS)], r1.at[pl.ds(place_in_order * ROWS, ROWS)], send_sem.at[0], recv_sem.at[0],
            device_id=(to // GY, lax.rem(to, GY)), device_id_type=MESH).start()
        return c

    lax.fori_loop(1, N, send1, 0)
    own1 = pltpu.make_async_copy(
        s1.at[pl.ds(plane * ROWS, ROWS)], r1.at[pl.ds(place_in_order * ROWS, ROWS)], own_sem.at[0])
    own1.start()

    lax.fori_loop(EARLY, 15, look_wide, 0)
    lax.fori_loop(15, 32, look_narrow, 0)
    look_up(32, TABLE)
    lax.fori_loop(33, 36, look_wide, 0)

    xfh, xfl = bases[1, 0], bases[1, 1]
    all_but_one = pl.ds(0, (N - 1) * ROWS)
    got = r1.at[all_but_one]
    pltpu.make_async_copy(got, got, recv_sem.at[0]).wait()
    own1.wait()
    for g in range(GY):
        block = jnp.concatenate([r1[pl.ds(g * GX * ROWS + x, GX, stride=ROWS), :] for x in range(8)], axis=0)
        mid[g] = mm3((xfh, xfl), split(block))
    for h in range(2):
        ends = [jnp.concatenate([r1[pl.ds((2 * a + h) * GX * ROWS + 8 + r, GX, stride=ROWS), :] for r in range(2)], axis=0)
                for a in range(4)]
        mid[8 + h] = mm3((xfh, xfl), split(jnp.concatenate(exchange(ends, 32), axis=0)))

    def regroup(tile, c):
        place = pl.ds(pl.multiple_of(tile * 32, 32), 32)
        main = exchange([mid[i, place] for i in range(8)], 16)
        ends = exchange([mid[i, place] for i in (8, 9)], 16)
        for i, value in enumerate(main + ends):
            mid[i, place] = value
        return c

    lax.fori_loop(0, 4, regroup, 0)

    ybh, ybl = bases[4, 0], bases[4, 1]
    for q in range(Q):
        spec[q] = mm3(split(mid[q]), (ybh, ybl)).reshape(2, HALF, N)

    to_sibling = pltpu.make_async_remote_copy(
        spec.at[:, :, pl.ds((1 - core) * 32, 32)], partner, sib_sem.at[0], sib_sem.at[1],
        device_id=(gx, sib), device_id_type=MESH)
    to_sibling.start()

    def contract(tile, energy):
        parity = tile // 8
        place = pl.ds(pl.multiple_of(lax.rem(tile, 8) * 8, 8), 8)
        krow = jnp.where(tile == 8, HALF, lax.rem(tile, 8) * 8)
        s = [spec[q, parity, place] for q in range(Q)]
        for q in range(Q):
            acc = None
            for p in range(Q):
                term = ktab[pl.ds(pl.multiple_of((q * Q + p) * KROWS + krow, 8), 8), :] * s[p]
                acc = term if acc is None else acc + term
            uspec[q, parity, place] = acc
            energy = energy + acc * s[q]
        return energy

    zero = jnp.zeros((8, N), F32)
    energy = lax.fori_loop(0, 16, contract, zero)

    yfh, yfl = bases[3, 0], bases[3, 1]
    for q in range(Q):
        mid[q] = mm3(split(uspec[q].reshape(N, N)), (yfh, yfl))
    lax.fori_loop(0, 4, regroup, 0)

    xbh, xbl = bases[2, 0], bases[2, 1]
    for g in range(GY):
        block = mm3((xbh, xbl), split(mid[g]))
        for x in range(8):
            s2[pl.ds(g * GX * ROWS + x, GX, stride=ROWS), :] = block[x * GX:(x + 1) * GX]
    for h in range(2):
        block = mm3((xbh, xbl), split(mid[8 + h]))
        ends = exchange([block[b * 32:(b + 1) * 32] for b in range(4)], 32)
        for a in range(4):
            for r in range(2):
                s2[pl.ds((2 * a + h) * GX * ROWS + 8 + r, GX, stride=ROWS), :] = ends[a][r * GX:(r + 1) * GX]

    def send2(i, c):
        to = lax.rem(plane + i, N)
        to_x, to_y = to // GY, lax.rem(to, GY)
        pltpu.make_async_remote_copy(
            s2.at[pl.ds((to_y * GX + to_x) * ROWS, ROWS)], r2.at[pl.ds(plane * ROWS, ROWS)], send_sem.at[1], recv_sem.at[1],
            device_id=(to_x, to_y), device_id_type=MESH).start()
        return c

    lax.fori_loop(1, FIRST, send2, 0)
    own2 = pltpu.make_async_copy(
        s2.at[pl.ds(place_in_order * ROWS, ROWS)], r2.at[pl.ds(plane * ROWS, ROWS)], own_sem.at[1])
    own2.start()

    lane = lanes_iota(8)
    sub = lax.broadcasted_iota(jnp.int32, (8, N), 0)
    j = lane & (HALF - 1)
    ky_off = j.astype(F32)
    ky_full = jnp.where(lane == HALF, HALF, j).astype(F32)
    sy = lane // HALF
    ynyq = lane == HALF
    top = float(HALF * HALF)
    kz_f = kz.astype(F32)
    kz_off = kz_low.astype(F32)

    def moments(tile, sums):
        parity = tile // 8
        place = pl.ds(pl.multiple_of(lax.rem(tile, 8) * 8, 8), 8)
        krow = jnp.where(tile == 8, HALF, lax.rem(tile, 8) * 8)
        s = [spec[q, parity, place] for q in range(Q)]
        weight = zero
        cross = zero
        for q in range(Q):
            acc = None
            for p in range(Q):
                term = ktab[pl.ds(pl.multiple_of(sym_index(q, p) * KROWS + krow, 8), 8), :] * s[p]
                acc = term if acc is None else acc + term
            grad[q, parity, place] = acc
            weight = weight + acc * s[q]
            cross = cross + acc * pltpu.roll(spec[q, 1 - parity, place], HALF, 1)
        i = lax.rem(tile, 8) * 8 + sub
        kx_off = i.astype(F32)
        xnyq = (i == 0) & (parity == 1)
        kx_full = jnp.where(xnyq, top, kx_off * kx_off)
        xx, yy, zz, xy, xz, yz = sums
        xx = xx + weight * kx_full
        yy = yy + weight * (ky_full * ky_full)
        zz = zz + weight
        sign = jnp.where(sy == parity, -1.0, 1.0)
        xy = xy + cross * (sign * kx_off * ky_off) + jnp.where(xnyq & ynyq, weight * top, 0.0)
        xz = xz + jnp.where(xnyq & is_znyq, weight * top, 0.0)
        yz = yz + jnp.where(ynyq & is_znyq, weight * top, 0.0)
        return xx, yy, zz, xy, xz, yz

    xx, yy, zz, xy, xz, yz = lax.fori_loop(0, 16, moments, (zero,) * 6)

    to_sibling.wait()

    def mixed(step, sums):
        parity = step // 4
        here = lax.rem(step, 4) * 8
        mine = pl.ds(pl.multiple_of(core * 32 + here, 8), 8)
        theirs = pl.ds(pl.multiple_of(here, 8), 8)
        along_x = zero
        along_y = zero
        for q in range(Q):
            g = grad[q, parity, mine]
            along_x = along_x + g * partner[q, 1 - parity, theirs]
            along_y = along_y + g * pltpu.roll(partner[q, parity, theirs], HALF, 1)
        kx_off = (core * 32 + here + sub).astype(F32)
        xz, yz = sums
        xz = xz + along_x * (jnp.where(parity == core, -2.0, 2.0) * kz_off * kx_off)
        yz = yz + along_y * (jnp.where(sy == core, -2.0, 2.0) * kz_off * ky_off)
        return xz, yz

    xz, yz = lax.fori_loop(0, 8, mixed, (xz, yz))
    zz = zz * (kz_f * kz_f)
    part[...] = zero
    for row, total in enumerate((energy, xx, yy, zz, xy, xz, yz)):
        part[pl.ds(row, 1)] = jnp.sum(total, axis=0, keepdims=True)
    sums_a[gy] = part[...]

    def send_sum_y(i, k):
        to = lax.rem(gy + i, GY)
        pltpu.make_async_remote_copy(part, sums_a.at[gy], send_sem.at[2], sum_sem.at[0],
                                     device_id=(gx, to), device_id_type=MESH).start()
        return k

    lax.fori_loop(1, GY, send_sum_y, 0)
    lax.fori_loop(FIRST, N, send2, 0)

    got = sums_a.at[pl.ds(0, GY - 1)]
    pltpu.make_async_copy(got, got, sum_sem.at[0]).wait()
    total = sums_a[0]
    for i in range(1, GY):
        total = total + sums_a[i]
    sums_b[gx] = total

    def send_sum_x(i, k):
        to = lax.rem(gx + i, GX)
        pltpu.make_async_remote_copy(sums_b.at[gx], sums_b.at[gx], send_sem.at[3], sum_sem.at[1],
                                     device_id=(to, gy), device_id_type=MESH).start()
        return k

    lax.fori_loop(1, GX, send_sum_x, 0)

    got = sums_b.at[pl.ds(0, GX - 1)]
    pltpu.make_async_copy(got, got, sum_sem.at[1]).wait()
    total = sums_b[0]
    for i in range(1, GX):
        total = total + sums_b[i]
    cells = float(N) ** 3
    wave = (2.0 * math.pi / N) ** 2
    sums = jnp.sum(total, axis=1, keepdims=True)
    row = lax.broadcasted_iota(jnp.int32, (8, 1), 0)

    def pick_sum(r):
        return jnp.sum(jnp.where(row == r, sums, 0.0), axis=0, keepdims=True)

    energy_out[...] = pick_sum(0) * (0.5 / cells)
    r3 = lax.broadcasted_iota(jnp.int32, (3, 3), 0)
    c3 = lax.broadcasted_iota(jnp.int32, (3, 3), 1)
    stress = jnp.zeros((3, 3), F32)
    for r, (a, b) in enumerate(((0, 0), (1, 1), (2, 2), (0, 1), (0, 2), (1, 2))):
        here = ((r3 == a) & (c3 == b)) | ((r3 == b) & (c3 == a))
        stress = jnp.where(here, pick_sum(r + 1) * (-0.5 * wave / cells), stress)
    stress_out[...] = stress

    got = r2.at[all_but_one]
    pltpu.make_async_copy(got, got, recv_sem.at[1]).wait()
    own2.wait()
    for x in range(8):
        block = r2[pl.ds(x, N, stride=ROWS), :].T
        u_out[0:8, x] = mm3(split(block), (zbh, zbl)).reshape(8, 16, N)
    for r in range(2):
        block = r2[pl.ds(8 + r, N, stride=ROWS), :].T
        out = mm3(split(block), (zbh, zbl)).reshape(4, 2, 16, N)
        for b in range(4):
            for q in range(2):
                u_out[8 + q, 2 * b + r] = out[b, q]

    for slot, buffer in ((0, s1.at[all_but_one]), (1, s2.at[all_but_one]),
                         (2, sums_a.at[pl.ds(0, GY - 1)]), (3, sums_b.at[pl.ds(0, GX - 1)])):
        pltpu.make_async_copy(buffer, buffer, send_sem.at[slot]).wait()


def shards(theta, phi, dphi):
    vmem = pl.BlockSpec(memory_space=pltpu.VMEM)
    cube = pltpu.VMEM((Q, N, N), F32)
    halves_cube = pltpu.VMEM((Q, 2, HALF, N), F32)
    rows = pltpu.VMEM((N * ROWS, N), F32)
    u, stress, energy = pl.pallas_call(
        kernel,
        out_shape=(
            jax.ShapeDtypeStruct((Q, 8, 16, N), F32),
            jax.ShapeDtypeStruct((3, 3), F32),
            jax.ShapeDtypeStruct((1, 1), F32),
        ),
        in_specs=[pl.BlockSpec(memory_space=pl.ANY)] * 5,
        out_specs=(vmem,) * 3,
        scratch_shapes=[
            pltpu.VMEM((Q, 8, 16, N), F32),
            pltpu.VMEM((Q * Q, TABLE), F32),
            pltpu.VMEM((Q * Q, TABLE), F32),
            pltpu.VMEM((5, 2, N, N), BF16),
            pltpu.VMEM((2, PAIRS, Q * Q), BF16),
            rows, rows, rows, rows, cube, halves_cube, halves_cube, halves_cube,
            pltpu.VMEM((Q, 2, 32, N), F32),
            pltpu.VMEM((PAIRS * KROWS, N), F32),
            pltpu.VMEM((4 * PAIRS, TABLE), BF16),
            pltpu.VMEM((GY, 8, N), F32),
            pltpu.VMEM((GX, 8, N), F32),
            pltpu.VMEM((8, N), F32),
            pltpu.SemaphoreType.DMA((4,)),
            pltpu.SemaphoreType.DMA((2,)),
            pltpu.SemaphoreType.DMA((2,)),
            pltpu.SemaphoreType.DMA((2,)),
            pltpu.SemaphoreType.DMA((2,)),
            pltpu.SemaphoreType.DMA((5,)),
        ],
        compiler_params=pltpu.CompilerParams(
            collective_id=0, has_side_effects=True, vmem_limit_bytes=56 << 20),
    )(theta, phi.T, dphi.T, *(jnp.asarray(c) for c in constants()))
    return u, stress, energy.reshape(())


def solution(mesh):
    return jax.shard_map(
        shards,
        mesh=mesh,
        in_specs=(P(None, "gx", "gy", None), P(), P()),
        out_specs=(P(None, "gx", "gy", None), P(), P()),
        check_vma=False,
    )
```

```python
import functools
import math

import jax
import jax.numpy as jnp
import ml_dtypes
import numpy as np
from jax import lax
from jax.experimental import pallas as pl
from jax.experimental.pallas import tpu as pltpu
from jax.sharding import PartitionSpec as P

MESH = pl.DeviceIdType.MESH
F32 = jnp.float32
BF16 = jnp.bfloat16
N = 128
HALF = 64
Q = 10
GX = 16
REGROUP = 128
FIRST, SECOND = 64, 96
GY = 8
ROWS = 10
VALUES = 104
SLOPES = 56
PAIRS = Q * Q + SLOPES
GROUPS = 9
SPLIT = 4
TABLE = 1024


def real_basis():
    r = np.arange(N)
    rows = [np.full(N, 1.0) / np.sqrt(N)]
    rows += [np.cos(2 * np.pi * k * r / N) * np.sqrt(2.0 / N) for k in range(1, HALF)]
    rows += [np.cos(np.pi * r) / np.sqrt(N)]
    rows += [np.sin(2 * np.pi * k * r / N) * np.sqrt(2.0 / N) for k in range(1, HALF)]
    return np.array(rows)


def halves(array):
    high = array.astype(ml_dtypes.bfloat16)
    low = (array - high.astype(np.float64)).astype(ml_dtypes.bfloat16)
    return np.stack([high, low])


def sym_index(q, p):
    q, p = min(q, p), max(q, p)
    return 100 + q * Q - q * (q - 1) // 2 + (p - q)


def constants():
    basis = real_basis()
    order = np.array([(lane // 2) + HALF * (lane % 2) for lane in range(N)])
    z_basis = basis[order]
    by_source = np.array([(i % GX) * 8 + i // GX for i in range(N)])
    x_basis = basis[:, by_source]
    pick = np.zeros((SLOPES, Q * Q))
    for q in range(Q):
        for p in range(q, Q):
            pick[sym_index(q, p) - Q * Q, q * Q + p] += 0.5
            pick[sym_index(q, p) - Q * Q, p * Q + q] += 0.5
    bases = np.stack([halves(b) for b in (z_basis, x_basis, x_basis.T, basis, basis.T)])
    return bases, pick.astype(ml_dtypes.bfloat16)


def split(value):
    high = value.astype(BF16)
    return high, (value - high.astype(F32)).astype(BF16)


def mm(a, b, dims=(((1,), (0,)), ((), ()))):
    return lax.dot_general(a, b, dims, preferred_element_type=F32)


def mm3(a, b, dims=(((1,), (0,)), ((), ()))):
    (ah, al), (bh, bl) = a, b
    return mm(ah, bh, dims) + (mm(al, bh, dims) + mm(ah, bl, dims))


def lanes_iota(rows):
    return lax.broadcasted_iota(jnp.int32, (rows, N), 1)


def exchange(values, lane_step):
    values = list(values)
    axis = values[0].ndim - 1
    lane = lax.broadcasted_iota(jnp.int32, values[0].shape, axis)
    bit = 1
    while bit < len(values):
        step = bit * lane_step
        low = (lane & step) == 0
        for i in range(len(values)):
            if i & bit:
                continue
            first, second = values[i], values[i | bit]
            values[i] = jnp.where(low, first, pltpu.roll(second, step, axis))
            values[i | bit] = jnp.where(low, pltpu.roll(first, N - step, axis), second)
        bit *= 2
    return values


def kernel(theta_in, phi_in, dphi_in, bases_in, pick_in, r2, total_out,
           theta, phi, dphi, bases, pick, s1, r1, s2, mid, spec, uspec, grad, partner, ktab, tabs, sums_a, sums_b, part,
           send_sem, recv_sem, own_sem, sib_sem, sum_sem, in_sem, tab_sem):
    inputs = [pltpu.make_async_copy(source, target, in_sem.at[i]) for i, (source, target) in enumerate(
        ((theta_in, theta), (bases_in, bases), (phi_in, phi), (dphi_in, dphi), (pick_in, pick)))]
    for copy in inputs:
        copy.start()
    gx = lax.axis_index("gx")
    gy = lax.axis_index("gy")
    core = lax.rem(gy, 2)
    plane = gx * GY + gy
    place_in_order = gy * GX + gx
    kz_low = plane // 2
    is_znyq = plane == 1
    kz = jnp.where(is_znyq, HALF, kz_low)
    sib = gy + 1 - 2 * core

    barrier = pltpu.get_barrier_semaphore()

    def hello(i, c):
        to = lax.rem(plane + i, N)
        pl.semaphore_signal(barrier, inc=1, device_id=(to // GY, lax.rem(to, GY)), device_id_type=MESH)
        return c

    lax.fori_loop(1, N, hello, 0)

    nt = (((1,), (1,)), ((), ()))
    inputs[0].wait()
    inputs[1].wait()
    zbh, zbl = bases[0, 0], bases[0, 1]
    for x in range(8):
        block = theta[0:8, x].reshape(N, N)
        s1[pl.ds(x, N, stride=ROWS), :] = mm3((zbh, zbl), split(block), nt)
    for r in range(2):
        block = jnp.concatenate([theta[8 + q, 2 * b + r] for b in range(4) for q in range(2)], axis=0)
        s1[pl.ds(8 + r, N, stride=ROWS), :] = mm3((zbh, zbl), split(block), nt)

    for copy in inputs[2:]:
        copy.wait()

    def halves_of(table, first):
        difference = pltpu.roll(table, TABLE - 1, 1) - table
        parts = []
        for value in (table, difference):
            high = value.astype(BF16).astype(F32)
            parts += [high, value - high]
        tabs[first:first + 4 * table.shape[0]] = jnp.concatenate(parts, axis=0).astype(BF16)

    def prepare():
        halves_of(jnp.concatenate([phi[...], jnp.zeros((VALUES - Q * Q, TABLE), F32)], axis=0), 0)
        dphi_h, dphi_l = split(dphi[...])
        halves_of(mm(pick[...], dphi_h) + mm(pick[...], dphi_l), 4 * VALUES)

    lane256 = lax.broadcasted_iota(jnp.int32, (1, 2 * N), 1)
    ky256 = jnp.where(lax.rem(lane256, N) == HALF, HALF, lane256 & (HALF - 1))
    second256 = lane256 // N

    def look_up(step, width):
        row = 2 * step
        first = jnp.where(row > HALF, row - HALF, row)
        near = first * first + kz * kz
        first_tile = 0
        if width < TABLE:
            for t in range(1, (TABLE - width) // N + 1):
                first_tile = first_tile + jnp.minimum(near // math.ceil(t * t * 128.0 * 128.0 * 3 * 4096 / (1023.0 * 1023.0)), 1)
        base = pl.multiple_of(first_tile * N, N)
        kx = row + second256
        kx = jnp.where(kx > HALF, kx - HALF, kx)
        square = kx * kx + ky256 * ky256 + kz * kz
        radial = jnp.sqrt(square.astype(F32)) * ((TABLE - 1) / (HALF * math.sqrt(3.0)))
        lower = jnp.clip(jnp.floor(radial), 0.0, TABLE - 2.0)
        fraction = radial - lower
        index = lower.astype(jnp.int32) - first_tile * N
        points = lax.broadcasted_iota(jnp.int32, (width, 2 * N), 0)
        onehot = jnp.where(points == index, 1.0, 0.0).astype(BF16)
        out = mm(tabs[:, pl.ds(base, width)], onehot)
        for first, count, pair in ((0, VALUES, 0), (4 * VALUES, SLOPES, Q * Q)):
            part = [out[first + i * count:first + (i + 1) * count] for i in range(4)]
            value = (part[0] + part[1]) + fraction * (part[2] + part[3])
            start = (row // 8 * PAIRS + pair) * 8 + row % 8
            ktab[pl.ds(start, count, stride=8), :] = value[:, 0:N]
            ktab[pl.ds(start + 1, count, stride=8), :] = value[:, N:]

    def wide(step, k):
        look_up(step, 768)
        return k

    def narrow(step, k):
        look_up(step, 512)
        return k

    def last(step, k):
        look_up(step, TABLE)
        return k

    def piece(group, slope):
        return ktab.at[pl.ds((group * PAIRS + slope * Q * Q) * 8, (SLOPES if slope else Q * Q) * 8)]

    def share(group, slope):
        mine = piece(group, slope)
        return pltpu.make_async_remote_copy(mine, mine, tab_sem.at[0, slope, group], tab_sem.at[1, slope, group],
                                            device_id=(gx, sib), device_id_type=MESH)

    owned = (range(SPLIT), range(SPLIT, GROUPS))

    def look_group(group):
        for first, until, body in ((0, 15, wide), (15, 32, narrow), (32, 33, last), (33, 36, wide)):
            first, until = max(first, group * 4), min(until, group * 4 + 4)
            if first < until:
                lax.fori_loop(first, until, body, 0)

    shares = plane > 1

    @pl.when(plane <= 1)
    def _():
        prepare()
        for owner in (0, 1):
            @pl.when(core == owner)
            def _(owner=owner):
                for group in owned[1 - owner]:
                    look_group(group)

    pl.semaphore_wait(barrier, N - 1)

    def send1(i, c):
        to = lax.rem(plane + i, N)
        pltpu.make_async_remote_copy(
            s1.at[pl.ds(to * ROWS, ROWS)], r1.at[pl.ds(place_in_order * ROWS, ROWS)], send_sem.at[0], recv_sem.at[0],
            device_id=(to // GY, lax.rem(to, GY)), device_id_type=MESH).start()
        return c

    lax.fori_loop(1, N, send1, 0)
    own1 = pltpu.make_async_copy(
        s1.at[pl.ds(plane * ROWS, ROWS)], r1.at[pl.ds(place_in_order * ROWS, ROWS)], own_sem.at[0])
    own1.start()

    @pl.when(shares)
    def _():
        prepare()

    for owner in (0, 1):
        @pl.when(core == owner)
        def _(owner=owner):
            for group in owned[owner]:
                look_group(group)

                @pl.when(shares)
                def _(group=group):
                    share(group, 0).start()
                    share(group, 1).start()

            @pl.when(shares)
            def _():
                for group in owned[1 - owner]:
                    theirs = piece(group, 0)
                    pltpu.make_async_copy(theirs, theirs, tab_sem.at[1, 0, group]).wait()

    xfh, xfl = bases[1, 0], bases[1, 1]
    all_but_one = pl.ds(0, (N - 1) * ROWS)
    got = r1.at[all_but_one]
    pltpu.make_async_copy(got, got, recv_sem.at[0]).wait()
    own1.wait()
    for g in range(GY):
        block = jnp.concatenate([r1[pl.ds(g * GX * ROWS + x, GX, stride=ROWS), :] for x in range(8)], axis=0)
        mid[g] = mm3((xfh, xfl), split(block))
    for h in range(2):
        ends = [jnp.concatenate([r1[pl.ds((2 * a + h) * GX * ROWS + 8 + r, GX, stride=ROWS), :] for r in range(2)], axis=0)
                for a in range(4)]
        mid[8 + h] = mm3((xfh, xfl), split(jnp.concatenate(exchange(ends, 32), axis=0)))

    def regroup(tile, c):
        place = pl.ds(pl.multiple_of(tile * REGROUP, REGROUP), REGROUP)
        main = exchange([mid[i, place] for i in range(8)], 16)
        ends = exchange([mid[i, place] for i in (8, 9)], 16)
        for i, value in enumerate(main + ends):
            mid[i, place] = value
        return c

    lax.fori_loop(0, N // REGROUP, regroup, 0)

    ybh, ybl = bases[4, 0], bases[4, 1]
    for q in range(Q):
        spec[q] = mm3(split(mid[q]), (ybh, ybl)).reshape(2, HALF, N)

    to_sibling = pltpu.make_async_remote_copy(
        spec.at[:, :, pl.ds((1 - core) * 32, 32)], partner, sib_sem.at[0], sib_sem.at[1],
        device_id=(gx, sib), device_id_type=MESH)
    to_sibling.start()

    def contract(tile, energy):
        parity = tile // 8
        place = pl.ds(pl.multiple_of(lax.rem(tile, 8) * 8, 8), 8)
        group = jnp.where(tile == 8, 8, lax.rem(tile, 8))
        s = [spec[q, parity, place] for q in range(Q)]
        for q in range(Q):
            acc = None
            for p in range(Q):
                term = ktab[pl.ds(pl.multiple_of((group * PAIRS + q * Q + p) * 8, 8), 8), :] * s[p]
                acc = term if acc is None else acc + term
            uspec[q, parity, place] = acc
            energy = energy + acc * s[q]
        return energy

    zero = jnp.zeros((8, N), F32)
    energy = lax.fori_loop(0, 16, contract, zero)

    yfh, yfl = bases[3, 0], bases[3, 1]
    for q in range(Q):
        mid[q] = mm3(split(uspec[q].reshape(N, N)), (yfh, yfl))
    lax.fori_loop(0, N // REGROUP, regroup, 0)

    xbh, xbl = bases[2, 0], bases[2, 1]
    for g in range(GY):
        block = mm3((xbh, xbl), split(mid[g]))
        for x in range(8):
            s2[pl.ds(g * GX * ROWS + x, GX, stride=ROWS), :] = block[x * GX:(x + 1) * GX]
    for h in range(2):
        block = mm3((xbh, xbl), split(mid[8 + h]))
        ends = exchange([block[b * 32:(b + 1) * 32] for b in range(4)], 32)
        for a in range(4):
            for r in range(2):
                s2[pl.ds((2 * a + h) * GX * ROWS + 8 + r, GX, stride=ROWS), :] = ends[a][r * GX:(r + 1) * GX]

    def send2(i, c):
        to = lax.rem(plane + i, N)
        to_x, to_y = to // GY, lax.rem(to, GY)
        pltpu.make_async_remote_copy(
            s2.at[pl.ds((to_y * GX + to_x) * ROWS, ROWS)], r2.at[pl.ds(plane * ROWS, ROWS)], send_sem.at[1], recv_sem.at[1],
            device_id=(to_x, to_y), device_id_type=MESH).start()
        return c

    lax.fori_loop(1, FIRST, send2, 0)
    own2 = pltpu.make_async_copy(
        s2.at[pl.ds(place_in_order * ROWS, ROWS)], r2.at[pl.ds(plane * ROWS, ROWS)], own_sem.at[1])
    own2.start()

    for owner in (0, 1):
        @pl.when(shares & (core == owner))
        def _(owner=owner):
            for group in owned[1 - owner]:
                theirs = piece(group, 1)
                pltpu.make_async_copy(theirs, theirs, tab_sem.at[1, 1, group]).wait()
            for group in owned[owner]:
                share(group, 0).wait_send()
                share(group, 1).wait_send()

    lane = lanes_iota(8)
    sub = lax.broadcasted_iota(jnp.int32, (8, N), 0)
    j = lane & (HALF - 1)
    ky_off = j.astype(F32)
    ky_full = jnp.where(lane == HALF, HALF, j).astype(F32)
    sy = lane // HALF
    ynyq = lane == HALF
    top = float(HALF * HALF)
    kz_f = kz.astype(F32)
    kz_off = kz_low.astype(F32)

    def moments(tile, sums):
        parity = tile // 8
        place = pl.ds(pl.multiple_of(lax.rem(tile, 8) * 8, 8), 8)
        group = jnp.where(tile == 8, 8, lax.rem(tile, 8))
        s = [spec[q, parity, place] for q in range(Q)]
        weight = zero
        cross = zero
        for q in range(Q):
            acc = None
            for p in range(Q):
                term = ktab[pl.ds(pl.multiple_of((group * PAIRS + sym_index(q, p)) * 8, 8), 8), :] * s[p]
                acc = term if acc is None else acc + term
            grad[q, parity, place] = acc
            weight = weight + acc * s[q]
            cross = cross + acc * pltpu.roll(spec[q, 1 - parity, place], HALF, 1)
        i = lax.rem(tile, 8) * 8 + sub
        kx_off = i.astype(F32)
        xnyq = (i == 0) & (parity == 1)
        kx_full = jnp.where(xnyq, top, kx_off * kx_off)
        xx, yy, zz, xy, xz, yz = sums
        xx = xx + weight * kx_full
        yy = yy + weight * (ky_full * ky_full)
        zz = zz + weight
        sign = jnp.where(sy == parity, -1.0, 1.0)
        xy = xy + cross * (sign * kx_off * ky_off) + jnp.where(xnyq & ynyq, weight * top, 0.0)
        xz = xz + jnp.where(xnyq & is_znyq, weight * top, 0.0)
        yz = yz + jnp.where(ynyq & is_znyq, weight * top, 0.0)
        return xx, yy, zz, xy, xz, yz

    xx, yy, zz, xy, xz, yz = lax.fori_loop(0, 16, moments, (zero,) * 6)

    to_sibling.wait()

    def mixed(step, sums):
        parity = step // 4
        here = lax.rem(step, 4) * 8
        mine = pl.ds(pl.multiple_of(core * 32 + here, 8), 8)
        theirs = pl.ds(pl.multiple_of(here, 8), 8)
        along_x = zero
        along_y = zero
        for q in range(Q):
            g = grad[q, parity, mine]
            along_x = along_x + g * partner[q, 1 - parity, theirs]
            along_y = along_y + g * pltpu.roll(partner[q, parity, theirs], HALF, 1)
        kx_off = (core * 32 + here + sub).astype(F32)
        xz, yz = sums
        xz = xz + along_x * (jnp.where(parity == core, -2.0, 2.0) * kz_off * kx_off)
        yz = yz + along_y * (jnp.where(sy == core, -2.0, 2.0) * kz_off * ky_off)
        return xz, yz

    xz, yz = lax.fori_loop(0, 8, mixed, (xz, yz))
    zz = zz * (kz_f * kz_f)
    part[...] = zero
    for row, total in enumerate((energy, xx, yy, zz, xy, xz, yz)):
        part[pl.ds(row, 1)] = jnp.sum(total, axis=0, keepdims=True)
    sums_a[gy] = part[...]

    def send_sum_y(i, k):
        to = lax.rem(gy + i, GY)
        pltpu.make_async_remote_copy(part, sums_a.at[gy], send_sem.at[2], sum_sem.at[0],
                                     device_id=(gx, to), device_id_type=MESH).start()
        return k

    lax.fori_loop(1, GY, send_sum_y, 0)
    lax.fori_loop(FIRST, SECOND, send2, 0)

    got = sums_a.at[pl.ds(0, GY - 1)]
    pltpu.make_async_copy(got, got, sum_sem.at[0]).wait()
    total = sums_a[0]
    for i in range(1, GY):
        total = total + sums_a[i]
    sums_b[gx] = total

    def send_sum_x(i, k):
        to = lax.rem(gx + i, GX)
        pltpu.make_async_remote_copy(sums_b.at[gx], sums_b.at[gx], send_sem.at[3], sum_sem.at[1],
                                     device_id=(to, gy), device_id_type=MESH).start()
        return k

    lax.fori_loop(1, GX, send_sum_x, 0)
    lax.fori_loop(SECOND, N, send2, 0)

    got = sums_b.at[pl.ds(0, GX - 1)]
    pltpu.make_async_copy(got, got, sum_sem.at[1]).wait()
    total = sums_b[0]
    for i in range(1, GX):
        total = total + sums_b[i]
    total_out[...] = total

    got = r2.at[all_but_one]
    pltpu.make_async_copy(got, got, recv_sem.at[1]).wait()
    own2.wait()

    for slot, buffer in ((0, s1.at[all_but_one]), (1, s2.at[all_but_one]),
                         (2, sums_a.at[pl.ds(0, GY - 1)]), (3, sums_b.at[pl.ds(0, GX - 1)])):
        pltpu.make_async_copy(buffer, buffer, send_sem.at[slot]).wait()


def finish(received, total_in, bases_in, u_out, stress_out, energy_out, rows_in, total, bases, u, in_sem, out_sem):
    inputs = [pltpu.make_async_copy(source, target, in_sem.at[i]) for i, (source, target) in enumerate(
        ((received, rows_in), (bases_in.at[0], bases), (total_in, total)))]
    for copy in inputs:
        copy.start()
    for copy in inputs:
        copy.wait()
    zbh, zbl = bases[0], bases[1]
    for r in range(2):
        block = rows_in[pl.ds(8 + r, N, stride=ROWS), :].T
        out = mm3(split(block), (zbh, zbl)).reshape(4, 2, 16, N)
        for b in range(4):
            for q in range(2):
                u[2 * b + r, 8 + q] = out[b, q]
    copies = []
    for x in range(8):
        block = rows_in[pl.ds(x, N, stride=ROWS), :].T
        u[x, 0:8] = mm3(split(block), (zbh, zbl)).reshape(8, 16, N)
        copies.append(pltpu.make_async_copy(u.at[x], u_out.at[:, x], out_sem.at[x]))
        copies[-1].start()

    cells = float(N) ** 3
    wave = (2.0 * math.pi / N) ** 2
    sums = jnp.sum(total[...], axis=1, keepdims=True)
    row = lax.broadcasted_iota(jnp.int32, (8, 1), 0)

    def pick_sum(r):
        return jnp.sum(jnp.where(row == r, sums, 0.0), axis=0, keepdims=True)

    energy_out[...] = pick_sum(0) * (0.5 / cells)
    r3 = lax.broadcasted_iota(jnp.int32, (3, 3), 0)
    c3 = lax.broadcasted_iota(jnp.int32, (3, 3), 1)
    stress = jnp.zeros((3, 3), F32)
    for r, (a, b) in enumerate(((0, 0), (1, 1), (2, 2), (0, 1), (0, 2), (1, 2))):
        here = ((r3 == a) & (c3 == b)) | ((r3 == b) & (c3 == a))
        stress = jnp.where(here, pick_sum(r + 1) * (-0.5 * wave / cells), stress)
    stress_out[...] = stress
    for copy in copies:
        copy.wait()


def shards(theta, phi, dphi):
    vmem = pl.BlockSpec(memory_space=pltpu.VMEM)
    free = pl.BlockSpec(memory_space=pl.ANY)
    halves_cube = pltpu.VMEM((Q, 2, HALF, N), F32)
    rows = pltpu.VMEM((N * ROWS, N), F32)
    bases, pick = (jnp.asarray(c) for c in constants())
    received, total = pl.pallas_call(
        kernel,
        out_shape=(
            jax.ShapeDtypeStruct((N * ROWS, N), F32),
            jax.ShapeDtypeStruct((8, N), F32),
        ),
        in_specs=[free] * 5,
        out_specs=(vmem,) * 2,
        scratch_shapes=[
            pltpu.VMEM((Q, 8, 16, N), F32),
            pltpu.VMEM((Q * Q, TABLE), F32),
            pltpu.VMEM((Q * Q, TABLE), F32),
            pltpu.VMEM((5, 2, N, N), BF16),
            pltpu.VMEM((SLOPES, Q * Q), BF16),
            rows, rows, rows, pltpu.VMEM((Q, N, N), F32), halves_cube, halves_cube, halves_cube,
            pltpu.VMEM((Q, 2, 32, N), F32),
            pltpu.VMEM((GROUPS * PAIRS * 8, N), F32),
            pltpu.VMEM((4 * PAIRS + 16, TABLE), BF16),
            pltpu.VMEM((GY, 8, N), F32),
            pltpu.VMEM((GX, 8, N), F32),
            pltpu.VMEM((8, N), F32),
            pltpu.SemaphoreType.DMA((4,)),
            pltpu.SemaphoreType.DMA((2,)),
            pltpu.SemaphoreType.DMA((2,)),
            pltpu.SemaphoreType.DMA((2,)),
            pltpu.SemaphoreType.DMA((2,)),
            pltpu.SemaphoreType.DMA((5,)),
            pltpu.SemaphoreType.DMA((2, 2, GROUPS)),
        ],
        compiler_params=pltpu.CompilerParams(
            collective_id=0, has_side_effects=True, vmem_limit_bytes=56 << 20),
    )(theta, phi.T, dphi.T, bases, pick)
    u, stress, energy = pl.pallas_call(
        finish,
        out_shape=(
            jax.ShapeDtypeStruct((Q, 8, 16, N), F32),
            jax.ShapeDtypeStruct((3, 3), F32),
            jax.ShapeDtypeStruct((1, 1), F32),
        ),
        in_specs=[free] * 3,
        out_specs=(free, vmem, vmem),
        scratch_shapes=[
            rows,
            pltpu.VMEM((8, N), F32),
            pltpu.VMEM((2, N, N), BF16),
            pltpu.VMEM((8, Q, 16, N), F32),
            pltpu.SemaphoreType.DMA((3,)),
            pltpu.SemaphoreType.DMA((8,)),
        ],
        compiler_params=pltpu.CompilerParams(vmem_limit_bytes=56 << 20),
    )(received, total, bases)
    return u, stress, energy.reshape(())


def solution(mesh):
    return jax.shard_map(
        shards,
        mesh=mesh,
        in_specs=(P(None, "gx", "gy", None), P(), P()),
        out_specs=(P(None, "gx", "gy", None), P(), P()),
        check_vma=False,
    )
```

```python
import functools
import math

import jax
import jax.numpy as jnp
import ml_dtypes
import numpy as np
from jax import lax
from jax.experimental import pallas as pl
from jax.experimental.pallas import tpu as pltpu
from jax.sharding import PartitionSpec as P

MESH = pl.DeviceIdType.MESH
F32 = jnp.float32
BF16 = jnp.bfloat16
N = 128
HALF = 64
Q = 10
GX = 16
REGROUP = 128
FIRST, SECOND = 64, 112
GY = 8
ROWS = 10
VALUES = 104
SLOPES = 56
PAIRS = Q * Q + SLOPES
GROUPS = 9
SPLIT = 4
TABLE = 1024


def real_basis():
    r = np.arange(N)
    rows = [np.full(N, 1.0) / np.sqrt(N)]
    rows += [np.cos(2 * np.pi * k * r / N) * np.sqrt(2.0 / N) for k in range(1, HALF)]
    rows += [np.cos(np.pi * r) / np.sqrt(N)]
    rows += [np.sin(2 * np.pi * k * r / N) * np.sqrt(2.0 / N) for k in range(1, HALF)]
    return np.array(rows)


def halves(array):
    high = array.astype(ml_dtypes.bfloat16)
    low = (array - high.astype(np.float64)).astype(ml_dtypes.bfloat16)
    return np.stack([high, low])


def sym_index(q, p):
    q, p = min(q, p), max(q, p)
    return 100 + q * Q - q * (q - 1) // 2 + (p - q)


def constants():
    basis = real_basis()
    order = np.array([(lane // 2) + HALF * (lane % 2) for lane in range(N)])
    z_basis = basis[order]
    by_source = np.array([(i % GX) * 8 + i // GX for i in range(N)])
    x_basis = basis[:, by_source]
    pick = np.zeros((SLOPES, Q * Q))
    for q in range(Q):
        for p in range(q, Q):
            pick[sym_index(q, p) - Q * Q, q * Q + p] += 0.5
            pick[sym_index(q, p) - Q * Q, p * Q + q] += 0.5
    bases = np.stack([halves(b) for b in (z_basis, x_basis, x_basis.T, basis, basis.T)])
    return bases, pick.astype(ml_dtypes.bfloat16)


def split(value):
    high = value.astype(BF16)
    return high, (value - high.astype(F32)).astype(BF16)


def mm(a, b, dims=(((1,), (0,)), ((), ()))):
    return lax.dot_general(a, b, dims, preferred_element_type=F32)


def mm3(a, b, dims=(((1,), (0,)), ((), ()))):
    (ah, al), (bh, bl) = a, b
    return mm(ah, bh, dims) + (mm(al, bh, dims) + mm(ah, bl, dims))


def lanes_iota(rows):
    return lax.broadcasted_iota(jnp.int32, (rows, N), 1)


def exchange(values, lane_step):
    values = list(values)
    axis = values[0].ndim - 1
    lane = lax.broadcasted_iota(jnp.int32, values[0].shape, axis)
    bit = 1
    while bit < len(values):
        step = bit * lane_step
        low = (lane & step) == 0
        for i in range(len(values)):
            if i & bit:
                continue
            first, second = values[i], values[i | bit]
            values[i] = jnp.where(low, first, pltpu.roll(second, step, axis))
            values[i | bit] = jnp.where(low, pltpu.roll(first, N - step, axis), second)
        bit *= 2
    return values


def kernel(theta_in, phi_in, dphi_in, bases_in, pick_in, r2, total_out,
           theta, phi, dphi, bases, pick, s1, r1, s2, mid, spec, uspec, grad, partner, ktab, tabs, sums_a, sums_b, part,
           send_sem, recv_sem, own_sem, sib_sem, sum_sem, in_sem, tab_sem):
    inputs = [pltpu.make_async_copy(source, target, in_sem.at[i]) for i, (source, target) in enumerate(
        ((theta_in, theta), (bases_in, bases), (phi_in, phi), (dphi_in, dphi), (pick_in, pick)))]
    for copy in inputs:
        copy.start()
    gx = lax.axis_index("gx")
    gy = lax.axis_index("gy")
    core = lax.rem(gy, 2)
    plane = gx * GY + gy
    place_in_order = gy * GX + gx
    kz_low = plane // 2
    is_znyq = plane == 1
    kz = jnp.where(is_znyq, HALF, kz_low)
    sib = gy + 1 - 2 * core

    barrier = pltpu.get_barrier_semaphore()

    def hello(i, c):
        to = lax.rem(plane + i, N)
        pl.semaphore_signal(barrier, inc=1, device_id=(to // GY, lax.rem(to, GY)), device_id_type=MESH)
        return c

    lax.fori_loop(1, N, hello, 0)

    nt = (((1,), (1,)), ((), ()))
    inputs[0].wait()
    inputs[1].wait()
    zbh, zbl = bases[0, 0], bases[0, 1]
    for x in range(8):
        block = theta[0:8, x].reshape(N, N)
        s1[pl.ds(x, N, stride=ROWS), :] = mm3((zbh, zbl), split(block), nt)
    for r in range(2):
        block = jnp.concatenate([theta[8 + q, 2 * b + r] for b in range(4) for q in range(2)], axis=0)
        s1[pl.ds(8 + r, N, stride=ROWS), :] = mm3((zbh, zbl), split(block), nt)

    for copy in inputs[2:]:
        copy.wait()

    def halves_of(table, first):
        difference = pltpu.roll(table, TABLE - 1, 1) - table
        parts = []
        for value in (table, difference):
            high = value.astype(BF16).astype(F32)
            parts += [high, value - high]
        tabs[first:first + 4 * table.shape[0]] = jnp.concatenate(parts, axis=0).astype(BF16)

    def prepare():
        halves_of(jnp.concatenate([phi[...], jnp.zeros((VALUES - Q * Q, TABLE), F32)], axis=0), 0)
        dphi_h, dphi_l = split(dphi[...])
        halves_of(mm(pick[...], dphi_h) + mm(pick[...], dphi_l), 4 * VALUES)

    lane256 = lax.broadcasted_iota(jnp.int32, (1, 2 * N), 1)
    ky256 = jnp.where(lax.rem(lane256, N) == HALF, HALF, lane256 & (HALF - 1))
    second256 = lane256 // N

    def look_up(step, width):
        row = 2 * step
        first = jnp.where(row > HALF, row - HALF, row)
        near = first * first + kz * kz
        first_tile = 0
        if width < TABLE:
            for t in range(1, (TABLE - width) // N + 1):
                first_tile = first_tile + jnp.minimum(near // math.ceil(t * t * 128.0 * 128.0 * 3 * 4096 / (1023.0 * 1023.0)), 1)
        base = pl.multiple_of(first_tile * N, N)
        kx = row + second256
        kx = jnp.where(kx > HALF, kx - HALF, kx)
        square = kx * kx + ky256 * ky256 + kz * kz
        radial = jnp.sqrt(square.astype(F32)) * ((TABLE - 1) / (HALF * math.sqrt(3.0)))
        lower = jnp.clip(jnp.floor(radial), 0.0, TABLE - 2.0)
        fraction = radial - lower
        index = lower.astype(jnp.int32) - first_tile * N
        points = lax.broadcasted_iota(jnp.int32, (width, 2 * N), 0)
        onehot = jnp.where(points == index, 1.0, 0.0).astype(BF16)
        out = mm(tabs[:, pl.ds(base, width)], onehot)
        for first, count, pair in ((0, VALUES, 0), (4 * VALUES, SLOPES, Q * Q)):
            part = [out[first + i * count:first + (i + 1) * count] for i in range(4)]
            value = (part[0] + part[1]) + fraction * (part[2] + part[3])
            start = (row // 8 * PAIRS + pair) * 8 + row % 8
            ktab[pl.ds(start, count, stride=8), :] = value[:, 0:N]
            ktab[pl.ds(start + 1, count, stride=8), :] = value[:, N:]

    def wide(step, k):
        look_up(step, 768)
        return k

    def narrow(step, k):
        look_up(step, 512)
        return k

    def last(step, k):
        look_up(step, TABLE)
        return k

    def piece(group, slope):
        return ktab.at[pl.ds((group * PAIRS + slope * Q * Q) * 8, (SLOPES if slope else Q * Q) * 8)]

    def share(group, slope):
        mine = piece(group, slope)
        return pltpu.make_async_remote_copy(mine, mine, tab_sem.at[0, slope, group], tab_sem.at[1, slope, group],
                                            device_id=(gx, sib), device_id_type=MESH)

    owned = (range(SPLIT), range(SPLIT, GROUPS))

    def look_group(group):
        for first, until, body in ((0, 15, wide), (15, 32, narrow), (32, 33, last), (33, 36, wide)):
            first, until = max(first, group * 4), min(until, group * 4 + 4)
            if first < until:
                lax.fori_loop(first, until, body, 0)

    shares = plane > 1

    @pl.when(plane <= 1)
    def _():
        prepare()
        for owner in (0, 1):
            @pl.when(core == owner)
            def _(owner=owner):
                for group in owned[1 - owner]:
                    look_group(group)

    pl.semaphore_wait(barrier, N - 1)

    def send1(i, c):
        to = lax.rem(plane + i, N)
        pltpu.make_async_remote_copy(
            s1.at[pl.ds(to * ROWS, ROWS)], r1.at[pl.ds(place_in_order * ROWS, ROWS)], send_sem.at[0], recv_sem.at[0],
            device_id=(to // GY, lax.rem(to, GY)), device_id_type=MESH).start()
        return c

    lax.fori_loop(1, N, send1, 0)
    own1 = pltpu.make_async_copy(
        s1.at[pl.ds(plane * ROWS, ROWS)], r1.at[pl.ds(place_in_order * ROWS, ROWS)], own_sem.at[0])
    own1.start()

    @pl.when(shares)
    def _():
        prepare()

    for owner in (0, 1):
        @pl.when(core == owner)
        def _(owner=owner):
            for group in owned[owner]:
                look_group(group)

                @pl.when(shares)
                def _(group=group):
                    share(group, 0).start()
                    share(group, 1).start()

            @pl.when(shares)
            def _():
                for group in owned[1 - owner]:
                    theirs = piece(group, 0)
                    pltpu.make_async_copy(theirs, theirs, tab_sem.at[1, 0, group]).wait()

    xfh, xfl = bases[1, 0], bases[1, 1]
    all_but_one = pl.ds(0, (N - 1) * ROWS)
    got = r1.at[all_but_one]
    pltpu.make_async_copy(got, got, recv_sem.at[0]).wait()
    own1.wait()
    for g in range(GY):
        block = jnp.concatenate([r1[pl.ds(g * GX * ROWS + x, GX, stride=ROWS), :] for x in range(8)], axis=0)
        mid[g] = mm3((xfh, xfl), split(block))
    for h in range(2):
        ends = [jnp.concatenate([r1[pl.ds((2 * a + h) * GX * ROWS + 8 + r, GX, stride=ROWS), :] for r in range(2)], axis=0)
                for a in range(4)]
        mid[8 + h] = mm3((xfh, xfl), split(jnp.concatenate(exchange(ends, 32), axis=0)))

    def regroup(tile, c):
        place = pl.ds(pl.multiple_of(tile * REGROUP, REGROUP), REGROUP)
        main = exchange([mid[i, place] for i in range(8)], 16)
        ends = exchange([mid[i, place] for i in (8, 9)], 16)
        for i, value in enumerate(main + ends):
            mid[i, place] = value
        return c

    lax.fori_loop(0, N // REGROUP, regroup, 0)

    ybh, ybl = bases[4, 0], bases[4, 1]
    for q in range(Q):
        spec[q] = mm3(split(mid[q]), (ybh, ybl)).reshape(2, HALF, N)

    to_sibling = pltpu.make_async_remote_copy(
        spec.at[:, :, pl.ds((1 - core) * 32, 32)], partner, sib_sem.at[0], sib_sem.at[1],
        device_id=(gx, sib), device_id_type=MESH)
    to_sibling.start()

    def contract(tile, energy):
        parity = tile // 8
        place = pl.ds(pl.multiple_of(lax.rem(tile, 8) * 8, 8), 8)
        group = jnp.where(tile == 8, 8, lax.rem(tile, 8))
        s = [spec[q, parity, place] for q in range(Q)]
        for q in range(Q):
            acc = None
            for p in range(Q):
                term = ktab[pl.ds(pl.multiple_of((group * PAIRS + q * Q + p) * 8, 8), 8), :] * s[p]
                acc = term if acc is None else acc + term
            uspec[q, parity, place] = acc
            energy = energy + acc * s[q]
        return energy

    zero = jnp.zeros((8, N), F32)
    energy = lax.fori_loop(0, 16, contract, zero)

    yfh, yfl = bases[3, 0], bases[3, 1]
    for q in range(Q):
        mid[q] = mm3(split(uspec[q].reshape(N, N)), (yfh, yfl))
    lax.fori_loop(0, N // REGROUP, regroup, 0)

    xbh, xbl = bases[2, 0], bases[2, 1]
    for g in range(GY):
        block = mm3((xbh, xbl), split(mid[g]))
        for x in range(8):
            s2[pl.ds(g * GX * ROWS + x, GX, stride=ROWS), :] = block[x * GX:(x + 1) * GX]
    for h in range(2):
        block = mm3((xbh, xbl), split(mid[8 + h]))
        ends = exchange([block[b * 32:(b + 1) * 32] for b in range(4)], 32)
        for a in range(4):
            for r in range(2):
                s2[pl.ds((2 * a + h) * GX * ROWS + 8 + r, GX, stride=ROWS), :] = ends[a][r * GX:(r + 1) * GX]

    def send2(i, c):
        to = lax.rem(plane + i, N)
        to_x, to_y = to // GY, lax.rem(to, GY)
        pltpu.make_async_remote_copy(
            s2.at[pl.ds((to_y * GX + to_x) * ROWS, ROWS)], r2.at[pl.ds(plane * ROWS, ROWS)], send_sem.at[1], recv_sem.at[1],
            device_id=(to_x, to_y), device_id_type=MESH).start()
        return c

    lax.fori_loop(1, FIRST, send2, 0)
    own2 = pltpu.make_async_copy(
        s2.at[pl.ds(place_in_order * ROWS, ROWS)], r2.at[pl.ds(plane * ROWS, ROWS)], own_sem.at[1])
    own2.start()

    for owner in (0, 1):
        @pl.when(shares & (core == owner))
        def _(owner=owner):
            for group in owned[1 - owner]:
                theirs = piece(group, 1)
                pltpu.make_async_copy(theirs, theirs, tab_sem.at[1, 1, group]).wait()
            for group in owned[owner]:
                share(group, 0).wait_send()
                share(group, 1).wait_send()

    lane = lanes_iota(8)
    sub = lax.broadcasted_iota(jnp.int32, (8, N), 0)
    j = lane & (HALF - 1)
    ky_off = j.astype(F32)
    ky_full = jnp.where(lane == HALF, HALF, j).astype(F32)
    sy = lane // HALF
    ynyq = lane == HALF
    top = float(HALF * HALF)
    kz_f = kz.astype(F32)
    kz_off = kz_low.astype(F32)

    def moments(tile, sums):
        parity = tile // 8
        place = pl.ds(pl.multiple_of(lax.rem(tile, 8) * 8, 8), 8)
        group = jnp.where(tile == 8, 8, lax.rem(tile, 8))
        s = [spec[q, parity, place] for q in range(Q)]
        weight = zero
        cross = zero
        for q in range(Q):
            acc = None
            for p in range(Q):
                term = ktab[pl.ds(pl.multiple_of((group * PAIRS + sym_index(q, p)) * 8, 8), 8), :] * s[p]
                acc = term if acc is None else acc + term
            grad[q, parity, place] = acc
            weight = weight + acc * s[q]
            cross = cross + acc * pltpu.roll(spec[q, 1 - parity, place], HALF, 1)
        i = lax.rem(tile, 8) * 8 + sub
        kx_off = i.astype(F32)
        xnyq = (i == 0) & (parity == 1)
        kx_full = jnp.where(xnyq, top, kx_off * kx_off)
        xx, yy, zz, xy, xz, yz = sums
        xx = xx + weight * kx_full
        yy = yy + weight * (ky_full * ky_full)
        zz = zz + weight
        sign = jnp.where(sy == parity, -1.0, 1.0)
        xy = xy + cross * (sign * kx_off * ky_off) + jnp.where(xnyq & ynyq, weight * top, 0.0)
        xz = xz + jnp.where(xnyq & is_znyq, weight * top, 0.0)
        yz = yz + jnp.where(ynyq & is_znyq, weight * top, 0.0)
        return xx, yy, zz, xy, xz, yz

    xx, yy, zz, xy, xz, yz = lax.fori_loop(0, 16, moments, (zero,) * 6)

    to_sibling.wait()

    def mixed(step, sums):
        parity = step // 4
        here = lax.rem(step, 4) * 8
        mine = pl.ds(pl.multiple_of(core * 32 + here, 8), 8)
        theirs = pl.ds(pl.multiple_of(here, 8), 8)
        along_x = zero
        along_y = zero
        for q in range(Q):
            g = grad[q, parity, mine]
            along_x = along_x + g * partner[q, 1 - parity, theirs]
            along_y = along_y + g * pltpu.roll(partner[q, parity, theirs], HALF, 1)
        kx_off = (core * 32 + here + sub).astype(F32)
        xz, yz = sums
        xz = xz + along_x * (jnp.where(parity == core, -2.0, 2.0) * kz_off * kx_off)
        yz = yz + along_y * (jnp.where(sy == core, -2.0, 2.0) * kz_off * ky_off)
        return xz, yz

    xz, yz = lax.fori_loop(0, 8, mixed, (xz, yz))
    zz = zz * (kz_f * kz_f)
    part[...] = zero
    for row, total in enumerate((energy, xx, yy, zz, xy, xz, yz)):
        part[pl.ds(row, 1)] = jnp.sum(total, axis=0, keepdims=True)
    sums_a[gy] = part[...]

    def send_sum_y(i, k):
        to = lax.rem(gy + i, GY)
        pltpu.make_async_remote_copy(part, sums_a.at[gy], send_sem.at[2], sum_sem.at[0],
                                     device_id=(gx, to), device_id_type=MESH).start()
        return k

    lax.fori_loop(1, GY, send_sum_y, 0)
    lax.fori_loop(FIRST, SECOND, send2, 0)

    got = sums_a.at[pl.ds(0, GY - 1)]
    pltpu.make_async_copy(got, got, sum_sem.at[0]).wait()
    total = sums_a[0]
    for i in range(1, GY):
        total = total + sums_a[i]
    sums_b[gx] = total

    def send_sum_x(i, k):
        to = lax.rem(gx + i, GX)
        pltpu.make_async_remote_copy(sums_b.at[gx], sums_b.at[gx], send_sem.at[3], sum_sem.at[1],
                                     device_id=(to, gy), device_id_type=MESH).start()
        return k

    lax.fori_loop(1, GX, send_sum_x, 0)
    lax.fori_loop(SECOND, N, send2, 0)

    got = sums_b.at[pl.ds(0, GX - 1)]
    pltpu.make_async_copy(got, got, sum_sem.at[1]).wait()
    total = sums_b[0]
    for i in range(1, GX):
        total = total + sums_b[i]
    total_out[...] = total

    got = r2.at[all_but_one]
    pltpu.make_async_copy(got, got, recv_sem.at[1]).wait()
    own2.wait()

    for slot, buffer in ((0, s1.at[all_but_one]), (1, s2.at[all_but_one]),
                         (2, sums_a.at[pl.ds(0, GY - 1)]), (3, sums_b.at[pl.ds(0, GX - 1)])):
        pltpu.make_async_copy(buffer, buffer, send_sem.at[slot]).wait()


def finish(received, total_in, bases_in, u_out, stress_out, energy_out, rows_in, total, bases, u, in_sem, out_sem):
    inputs = [pltpu.make_async_copy(source, target, in_sem.at[i]) for i, (source, target) in enumerate(
        ((received, rows_in), (bases_in.at[0], bases), (total_in, total)))]
    for copy in inputs:
        copy.start()
    for copy in inputs:
        copy.wait()
    zbh, zbl = bases[0], bases[1]
    for r in range(2):
        block = rows_in[pl.ds(8 + r, N, stride=ROWS), :].T
        out = mm3(split(block), (zbh, zbl)).reshape(4, 2, 16, N)
        for b in range(4):
            for q in range(2):
                u[2 * b + r, 8 + q] = out[b, q]
    copies = []
    for x in range(8):
        block = rows_in[pl.ds(x, N, stride=ROWS), :].T
        u[x, 0:8] = mm3(split(block), (zbh, zbl)).reshape(8, 16, N)
        copies.append(pltpu.make_async_copy(u.at[x], u_out.at[:, x], out_sem.at[x]))
        copies[-1].start()

    cells = float(N) ** 3
    wave = (2.0 * math.pi / N) ** 2
    sums = jnp.sum(total[...], axis=1, keepdims=True)
    row = lax.broadcasted_iota(jnp.int32, (8, 1), 0)

    def pick_sum(r):
        return jnp.sum(jnp.where(row == r, sums, 0.0), axis=0, keepdims=True)

    energy_out[...] = pick_sum(0) * (0.5 / cells)
    r3 = lax.broadcasted_iota(jnp.int32, (3, 3), 0)
    c3 = lax.broadcasted_iota(jnp.int32, (3, 3), 1)
    stress = jnp.zeros((3, 3), F32)
    for r, (a, b) in enumerate(((0, 0), (1, 1), (2, 2), (0, 1), (0, 2), (1, 2))):
        here = ((r3 == a) & (c3 == b)) | ((r3 == b) & (c3 == a))
        stress = jnp.where(here, pick_sum(r + 1) * (-0.5 * wave / cells), stress)
    stress_out[...] = stress
    for copy in copies:
        copy.wait()


def shards(theta, phi, dphi):
    vmem = pl.BlockSpec(memory_space=pltpu.VMEM)
    free = pl.BlockSpec(memory_space=pl.ANY)
    halves_cube = pltpu.VMEM((Q, 2, HALF, N), F32)
    rows = pltpu.VMEM((N * ROWS, N), F32)
    bases, pick = (jnp.asarray(c) for c in constants())
    received, total = pl.pallas_call(
        kernel,
        out_shape=(
            jax.ShapeDtypeStruct((N * ROWS, N), F32),
            jax.ShapeDtypeStruct((8, N), F32),
        ),
        in_specs=[free] * 5,
        out_specs=(free, vmem),
        scratch_shapes=[
            pltpu.VMEM((Q, 8, 16, N), F32),
            pltpu.VMEM((Q * Q, TABLE), F32),
            pltpu.VMEM((Q * Q, TABLE), F32),
            pltpu.VMEM((5, 2, N, N), BF16),
            pltpu.VMEM((SLOPES, Q * Q), BF16),
            rows, rows, rows, pltpu.VMEM((Q, N, N), F32), halves_cube, halves_cube, halves_cube,
            pltpu.VMEM((Q, 2, 32, N), F32),
            pltpu.VMEM((GROUPS * PAIRS * 8, N), F32),
            pltpu.VMEM((4 * PAIRS + 16, TABLE), BF16),
            pltpu.VMEM((GY, 8, N), F32),
            pltpu.VMEM((GX, 8, N), F32),
            pltpu.VMEM((8, N), F32),
            pltpu.SemaphoreType.DMA((4,)),
            pltpu.SemaphoreType.DMA((2,)),
            pltpu.SemaphoreType.DMA((2,)),
            pltpu.SemaphoreType.DMA((2,)),
            pltpu.SemaphoreType.DMA((2,)),
            pltpu.SemaphoreType.DMA((5,)),
            pltpu.SemaphoreType.DMA((2, 2, GROUPS)),
        ],
        compiler_params=pltpu.CompilerParams(
            collective_id=0, has_side_effects=True, vmem_limit_bytes=56 << 20),
    )(theta, phi.T, dphi.T, bases, pick)
    u, stress, energy = pl.pallas_call(
        finish,
        out_shape=(
            jax.ShapeDtypeStruct((Q, 8, 16, N), F32),
            jax.ShapeDtypeStruct((3, 3), F32),
            jax.ShapeDtypeStruct((1, 1), F32),
        ),
        in_specs=[free] * 3,
        out_specs=(free, vmem, vmem),
        scratch_shapes=[
            rows,
            pltpu.VMEM((8, N), F32),
            pltpu.VMEM((2, N, N), BF16),
            pltpu.VMEM((8, Q, 16, N), F32),
            pltpu.SemaphoreType.DMA((3,)),
            pltpu.SemaphoreType.DMA((8,)),
        ],
        compiler_params=pltpu.CompilerParams(vmem_limit_bytes=56 << 20),
    )(received, total, bases)
    return u, stress, energy.reshape(())


def solution(mesh):
    return jax.shard_map(
        shards,
        mesh=mesh,
        in_specs=(P(None, "gx", "gy", None), P(), P()),
        out_specs=(P(None, "gx", "gy", None), P(), P()),
        check_vma=False,
    )
```

```python
import functools
import math

import jax
import jax.numpy as jnp
import ml_dtypes
import numpy as np
from jax import lax
from jax.experimental import pallas as pl
from jax.experimental.pallas import tpu as pltpu
from jax.sharding import PartitionSpec as P

MESH = pl.DeviceIdType.MESH
F32 = jnp.float32
BF16 = jnp.bfloat16
N = 128
HALF = 64
Q = 10
GX = 16
REGROUP = 128
FIRST, SECOND = 64, 112
GY = 8
ROWS = 10
VALUES = 104
SLOPES = 56
PAIRS = Q * Q + SLOPES
GROUPS = 9
SPLIT = 4
TABLE = 1024


def real_basis():
    r = np.arange(N)
    rows = [np.full(N, 1.0) / np.sqrt(N)]
    rows += [np.cos(2 * np.pi * k * r / N) * np.sqrt(2.0 / N) for k in range(1, HALF)]
    rows += [np.cos(np.pi * r) / np.sqrt(N)]
    rows += [np.sin(2 * np.pi * k * r / N) * np.sqrt(2.0 / N) for k in range(1, HALF)]
    return np.array(rows)


def halves(array):
    high = array.astype(ml_dtypes.bfloat16)
    low = (array - high.astype(np.float64)).astype(ml_dtypes.bfloat16)
    return np.stack([high, low])


def sym_index(q, p):
    q, p = min(q, p), max(q, p)
    return 100 + q * Q - q * (q - 1) // 2 + (p - q)


def constants():
    basis = real_basis()
    order = np.array([(lane // 2) + HALF * (lane % 2) for lane in range(N)])
    z_basis = basis[order]
    by_source = np.array([(i % GX) * 8 + i // GX for i in range(N)])
    x_basis = basis[:, by_source]
    pick = np.zeros((SLOPES, Q * Q))
    for q in range(Q):
        for p in range(q, Q):
            pick[sym_index(q, p) - Q * Q, q * Q + p] += 0.5
            pick[sym_index(q, p) - Q * Q, p * Q + q] += 0.5
    bases = np.stack([halves(b) for b in (z_basis, x_basis, x_basis.T, basis, basis.T)])
    return bases, pick.astype(ml_dtypes.bfloat16)


def split(value):
    high = value.astype(BF16)
    return high, (value - high.astype(F32)).astype(BF16)


def mm(a, b, dims=(((1,), (0,)), ((), ()))):
    return lax.dot_general(a, b, dims, preferred_element_type=F32)


def mm3(a, b, dims=(((1,), (0,)), ((), ()))):
    (ah, al), (bh, bl) = a, b
    return mm(ah, bh, dims) + (mm(al, bh, dims) + mm(ah, bl, dims))


def lanes_iota(rows):
    return lax.broadcasted_iota(jnp.int32, (rows, N), 1)


def exchange(values, lane_step):
    values = list(values)
    axis = values[0].ndim - 1
    lane = lax.broadcasted_iota(jnp.int32, values[0].shape, axis)
    bit = 1
    while bit < len(values):
        step = bit * lane_step
        low = (lane & step) == 0
        for i in range(len(values)):
            if i & bit:
                continue
            first, second = values[i], values[i | bit]
            values[i] = jnp.where(low, first, pltpu.roll(second, step, axis))
            values[i | bit] = jnp.where(low, pltpu.roll(first, N - step, axis), second)
        bit *= 2
    return values


def kernel(theta_in, phi_in, dphi_in, bases_in, pick_in, r2, total_out,
           theta, phi, dphi, bases, pick, s1, r1, s2, mid, spec, uspec, grad, partner, ktab, tabs, sums_a, sums_b, part,
           send_sem, recv_sem, own_sem, sib_sem, sum_sem, in_sem, tab_sem):
    inputs = [pltpu.make_async_copy(source, target, in_sem.at[i]) for i, (source, target) in enumerate(
        ((theta_in, theta), (bases_in, bases), (phi_in, phi), (dphi_in, dphi), (pick_in, pick)))]
    for copy in inputs:
        copy.start()
    gx = lax.axis_index("gx")
    gy = lax.axis_index("gy")
    core = lax.rem(gy, 2)
    plane = gx * GY + gy
    place_in_order = gy * GX + gx
    kz_low = plane // 2
    is_znyq = plane == 1
    kz = jnp.where(is_znyq, HALF, kz_low)
    sib = gy + 1 - 2 * core

    barrier = pltpu.get_barrier_semaphore()

    def hello(i, c):
        to = lax.rem(plane + i, N)
        pl.semaphore_signal(barrier, inc=1, device_id=(to // GY, lax.rem(to, GY)), device_id_type=MESH)
        return c

    lax.fori_loop(1, N, hello, 0)

    nt = (((1,), (1,)), ((), ()))
    inputs[0].wait()
    inputs[1].wait()
    zbh, zbl = bases[0, 0], bases[0, 1]
    for x in range(8):
        block = theta[0:8, x].reshape(N, N)
        s1[pl.ds(x, N, stride=ROWS), :] = mm3((zbh, zbl), split(block), nt)
    for r in range(2):
        block = jnp.concatenate([theta[8 + q, 2 * b + r] for b in range(4) for q in range(2)], axis=0)
        s1[pl.ds(8 + r, N, stride=ROWS), :] = mm3((zbh, zbl), split(block), nt)

    for copy in inputs[2:]:
        copy.wait()

    def halves_of(table, first):
        difference = pltpu.roll(table, TABLE - 1, 1) - table
        parts = []
        for value in (table, difference):
            high = value.astype(BF16).astype(F32)
            parts += [high, value - high]
        tabs[first:first + 4 * table.shape[0]] = jnp.concatenate(parts, axis=0).astype(BF16)

    def prepare():
        halves_of(jnp.concatenate([phi[...], jnp.zeros((VALUES - Q * Q, TABLE), F32)], axis=0), 0)
        dphi_h, dphi_l = split(dphi[...])
        halves_of(mm(pick[...], dphi_h) + mm(pick[...], dphi_l), 4 * VALUES)

    lane256 = lax.broadcasted_iota(jnp.int32, (1, 2 * N), 1)
    ky256 = jnp.where(lax.rem(lane256, N) == HALF, HALF, lane256 & (HALF - 1))
    second256 = lane256 // N

    def look_up(step, width):
        row = 2 * step
        first = jnp.where(row > HALF, row - HALF, row)
        near = first * first + kz * kz
        first_tile = 0
        if width < TABLE:
            for t in range(1, (TABLE - width) // N + 1):
                first_tile = first_tile + jnp.minimum(near // math.ceil(t * t * 128.0 * 128.0 * 3 * 4096 / (1023.0 * 1023.0)), 1)
        base = pl.multiple_of(first_tile * N, N)
        kx = row + second256
        kx = jnp.where(kx > HALF, kx - HALF, kx)
        square = kx * kx + ky256 * ky256 + kz * kz
        radial = jnp.sqrt(square.astype(F32)) * ((TABLE - 1) / (HALF * math.sqrt(3.0)))
        lower = jnp.clip(jnp.floor(radial), 0.0, TABLE - 2.0)
        fraction = radial - lower
        index = lower.astype(jnp.int32) - first_tile * N
        points = lax.broadcasted_iota(jnp.int32, (width, 2 * N), 0)
        onehot = jnp.where(points == index, 1.0, 0.0).astype(BF16)
        out = mm(tabs[:, pl.ds(base, width)], onehot)
        for first, count, pair in ((0, VALUES, 0), (4 * VALUES, SLOPES, Q * Q)):
            part = [out[first + i * count:first + (i + 1) * count] for i in range(4)]
            value = (part[0] + part[1]) + fraction * (part[2] + part[3])
            start = (row // 8 * PAIRS + pair) * 8 + row % 8
            ktab[pl.ds(start, count, stride=8), :] = value[:, 0:N]
            ktab[pl.ds(start + 1, count, stride=8), :] = value[:, N:]

    def wide(step, k):
        look_up(step, 768)
        return k

    def narrow(step, k):
        look_up(step, 512)
        return k

    def last(step, k):
        look_up(step, TABLE)
        return k

    def piece(group, slope):
        return ktab.at[pl.ds((group * PAIRS + slope * Q * Q) * 8, (SLOPES if slope else Q * Q) * 8)]

    def share(group, slope):
        mine = piece(group, slope)
        return pltpu.make_async_remote_copy(mine, mine, tab_sem.at[0, slope, group], tab_sem.at[1, slope, group],
                                            device_id=(gx, sib), device_id_type=MESH)

    owned = (range(SPLIT), range(SPLIT, GROUPS))

    def look_group(group):
        for first, until, body in ((0, 15, wide), (15, 32, narrow), (32, 33, last), (33, 36, wide)):
            first, until = max(first, group * 4), min(until, group * 4 + 4)
            if first < until:
                lax.fori_loop(first, until, body, 0)

    shares = plane > 1

    @pl.when(plane <= 1)
    def _():
        prepare()
        for owner in (0, 1):
            @pl.when(core == owner)
            def _(owner=owner):
                for group in owned[1 - owner]:
                    look_group(group)

    pl.semaphore_wait(barrier, N - 1)

    def send1(i, c):
        to = lax.rem(plane + i, N)
        pltpu.make_async_remote_copy(
            s1.at[pl.ds(to * ROWS, ROWS)], r1.at[pl.ds(place_in_order * ROWS, ROWS)], send_sem.at[0], recv_sem.at[0],
            device_id=(to // GY, lax.rem(to, GY)), device_id_type=MESH).start()
        return c

    lax.fori_loop(1, N, send1, 0)
    own1 = pltpu.make_async_copy(
        s1.at[pl.ds(plane * ROWS, ROWS)], r1.at[pl.ds(place_in_order * ROWS, ROWS)], own_sem.at[0])
    own1.start()

    @pl.when(shares)
    def _():
        prepare()

    for owner in (0, 1):
        @pl.when(core == owner)
        def _(owner=owner):
            for group in owned[owner]:
                look_group(group)

                @pl.when(shares)
                def _(group=group):
                    share(group, 0).start()
                    share(group, 1).start()

            @pl.when(shares)
            def _():
                for group in owned[1 - owner]:
                    theirs = piece(group, 0)
                    pltpu.make_async_copy(theirs, theirs, tab_sem.at[1, 0, group]).wait()

    xfh, xfl = bases[1, 0], bases[1, 1]
    all_but_one = pl.ds(0, (N - 1) * ROWS)
    got = r1.at[all_but_one]
    pltpu.make_async_copy(got, got, recv_sem.at[0]).wait()
    own1.wait()
    for g in range(GY):
        block = jnp.concatenate([r1[pl.ds(g * GX * ROWS + x, GX, stride=ROWS), :] for x in range(8)], axis=0)
        mid[g] = mm3((xfh, xfl), split(block))
    for h in range(2):
        ends = [jnp.concatenate([r1[pl.ds((2 * a + h) * GX * ROWS + 8 + r, GX, stride=ROWS), :] for r in range(2)], axis=0)
                for a in range(4)]
        mid[8 + h] = mm3((xfh, xfl), split(jnp.concatenate(exchange(ends, 32), axis=0)))

    def regroup(tile, c):
        place = pl.ds(pl.multiple_of(tile * REGROUP, REGROUP), REGROUP)
        main = exchange([mid[i, place] for i in range(8)], 16)
        ends = exchange([mid[i, place] for i in (8, 9)], 16)
        for i, value in enumerate(main + ends):
            mid[i, place] = value
        return c

    lax.fori_loop(0, N // REGROUP, regroup, 0)

    ybh, ybl = bases[4, 0], bases[4, 1]
    for q in range(Q):
        spec[q] = mm3(split(mid[q]), (ybh, ybl)).reshape(2, HALF, N)

    to_sibling = pltpu.make_async_remote_copy(
        spec.at[:, :, pl.ds((1 - core) * 32, 32)], partner, sib_sem.at[0], sib_sem.at[1],
        device_id=(gx, sib), device_id_type=MESH)
    to_sibling.start()

    def contract(tile, energy):
        parity = tile // 8
        place = pl.ds(pl.multiple_of(lax.rem(tile, 8) * 8, 8), 8)
        group = jnp.where(tile == 8, 8, lax.rem(tile, 8))
        s = [spec[q, parity, place] for q in range(Q)]
        for q in range(Q):
            acc = None
            for p in range(Q):
                term = ktab[pl.ds(pl.multiple_of((group * PAIRS + q * Q + p) * 8, 8), 8), :] * s[p]
                acc = term if acc is None else acc + term
            uspec[q, parity, place] = acc
            energy = energy + acc * s[q]
        return energy

    zero = jnp.zeros((8, N), F32)
    energy = lax.fori_loop(0, 16, contract, zero)

    yfh, yfl = bases[3, 0], bases[3, 1]
    for q in range(Q):
        mid[q] = mm3(split(uspec[q].reshape(N, N)), (yfh, yfl))
    lax.fori_loop(0, N // REGROUP, regroup, 0)

    xbh, xbl = bases[2, 0], bases[2, 1]
    for g in range(GY):
        block = mm3((xbh, xbl), split(mid[g]))
        for x in range(8):
            s2[pl.ds(g * GX * ROWS + x, GX, stride=ROWS), :] = block[x * GX:(x + 1) * GX]
    for h in range(2):
        block = mm3((xbh, xbl), split(mid[8 + h]))
        ends = exchange([block[b * 32:(b + 1) * 32] for b in range(4)], 32)
        for a in range(4):
            for r in range(2):
                s2[pl.ds((2 * a + h) * GX * ROWS + 8 + r, GX, stride=ROWS), :] = ends[a][r * GX:(r + 1) * GX]

    def send2(i, c):
        to = lax.rem(plane + i, N)
        to_x, to_y = to // GY, lax.rem(to, GY)
        pltpu.make_async_remote_copy(
            s2.at[pl.ds((to_y * GX + to_x) * ROWS, ROWS)], r2.at[pl.ds(plane * ROWS, ROWS)], send_sem.at[1], recv_sem.at[1],
            device_id=(to_x, to_y), device_id_type=MESH).start()
        return c

    lax.fori_loop(1, FIRST, send2, 0)
    own2 = pltpu.make_async_copy(
        s2.at[pl.ds(place_in_order * ROWS, ROWS)], r2.at[pl.ds(plane * ROWS, ROWS)], own_sem.at[1])
    own2.start()

    for owner in (0, 1):
        @pl.when(shares & (core == owner))
        def _(owner=owner):
            for group in owned[1 - owner]:
                theirs = piece(group, 1)
                pltpu.make_async_copy(theirs, theirs, tab_sem.at[1, 1, group]).wait()
            for group in owned[owner]:
                share(group, 0).wait_send()
                share(group, 1).wait_send()

    lane = lanes_iota(8)
    sub = lax.broadcasted_iota(jnp.int32, (8, N), 0)
    j = lane & (HALF - 1)
    ky_off = j.astype(F32)
    ky_full = jnp.where(lane == HALF, HALF, j).astype(F32)
    sy = lane // HALF
    ynyq = lane == HALF
    top = float(HALF * HALF)
    kz_f = kz.astype(F32)
    kz_off = kz_low.astype(F32)

    def moments(tile, sums):
        parity = tile // 8
        place = pl.ds(pl.multiple_of(lax.rem(tile, 8) * 8, 8), 8)
        group = jnp.where(tile == 8, 8, lax.rem(tile, 8))
        s = [spec[q, parity, place] for q in range(Q)]
        weight = zero
        cross = zero
        for q in range(Q):
            acc = None
            for p in range(Q):
                term = ktab[pl.ds(pl.multiple_of((group * PAIRS + sym_index(q, p)) * 8, 8), 8), :] * s[p]
                acc = term if acc is None else acc + term
            grad[q, parity, place] = acc
            weight = weight + acc * s[q]
            cross = cross + acc * pltpu.roll(spec[q, 1 - parity, place], HALF, 1)
        i = lax.rem(tile, 8) * 8 + sub
        kx_off = i.astype(F32)
        xnyq = (i == 0) & (parity == 1)
        kx_full = jnp.where(xnyq, top, kx_off * kx_off)
        xx, yy, zz, xy, xz, yz = sums
        xx = xx + weight * kx_full
        yy = yy + weight * (ky_full * ky_full)
        zz = zz + weight
        sign = jnp.where(sy == parity, -1.0, 1.0)
        xy = xy + cross * (sign * kx_off * ky_off) + jnp.where(xnyq & ynyq, weight * top, 0.0)
        xz = xz + jnp.where(xnyq & is_znyq, weight * top, 0.0)
        yz = yz + jnp.where(ynyq & is_znyq, weight * top, 0.0)
        return xx, yy, zz, xy, xz, yz

    xx, yy, zz, xy, xz, yz = lax.fori_loop(0, 16, moments, (zero,) * 6)

    to_sibling.wait()

    def mixed(step, sums):
        parity = step // 4
        here = lax.rem(step, 4) * 8
        mine = pl.ds(pl.multiple_of(core * 32 + here, 8), 8)
        theirs = pl.ds(pl.multiple_of(here, 8), 8)
        along_x = zero
        along_y = zero
        for q in range(Q):
            g = grad[q, parity, mine]
            along_x = along_x + g * partner[q, 1 - parity, theirs]
            along_y = along_y + g * pltpu.roll(partner[q, parity, theirs], HALF, 1)
        kx_off = (core * 32 + here + sub).astype(F32)
        xz, yz = sums
        xz = xz + along_x * (jnp.where(parity == core, -2.0, 2.0) * kz_off * kx_off)
        yz = yz + along_y * (jnp.where(sy == core, -2.0, 2.0) * kz_off * ky_off)
        return xz, yz

    xz, yz = lax.fori_loop(0, 8, mixed, (xz, yz))
    zz = zz * (kz_f * kz_f)
    part[...] = zero
    for row, total in enumerate((energy, xx, yy, zz, xy, xz, yz)):
        part[pl.ds(row, 1)] = jnp.sum(total, axis=0, keepdims=True)
    sums_a[gy] = part[...]

    def send_sum_y(i, k):
        to = lax.rem(gy + i, GY)
        pltpu.make_async_remote_copy(part, sums_a.at[gy], send_sem.at[2], sum_sem.at[0],
                                     device_id=(gx, to), device_id_type=MESH).start()
        return k

    lax.fori_loop(1, GY, send_sum_y, 0)
    lax.fori_loop(FIRST, SECOND, send2, 0)

    got = sums_a.at[pl.ds(0, GY - 1)]
    pltpu.make_async_copy(got, got, sum_sem.at[0]).wait()
    total = sums_a[0]
    for i in range(1, GY):
        total = total + sums_a[i]
    sums_b[gx] = total

    def send_sum_x(i, k):
        to = lax.rem(gx + i, GX)
        pltpu.make_async_remote_copy(sums_b.at[gx], sums_b.at[gx], send_sem.at[3], sum_sem.at[1],
                                     device_id=(to, gy), device_id_type=MESH).start()
        return k

    lax.fori_loop(1, GX, send_sum_x, 0)
    lax.fori_loop(SECOND, N, send2, 0)

    got = sums_b.at[pl.ds(0, GX - 1)]
    pltpu.make_async_copy(got, got, sum_sem.at[1]).wait()
    total = sums_b[0]
    for i in range(1, GX):
        total = total + sums_b[i]
    total_out[...] = total

    got = r2.at[all_but_one]
    pltpu.make_async_copy(got, got, recv_sem.at[1]).wait()
    own2.wait()

    for slot, buffer in ((0, s1.at[all_but_one]), (1, s2.at[all_but_one]),
                         (2, sums_a.at[pl.ds(0, GY - 1)]), (3, sums_b.at[pl.ds(0, GX - 1)])):
        pltpu.make_async_copy(buffer, buffer, send_sem.at[slot]).wait()


def finish(received, total_in, bases_in, u_out, stress_hbm, energy_hbm,
           rows_in, total, bases, u, stress_out, energy_out, in_sem, out_sem):
    inputs = [pltpu.make_async_copy(source, target, in_sem.at[i]) for i, (source, target) in enumerate(
        ((received, rows_in), (bases_in.at[0], bases), (total_in, total)))]
    for copy in inputs:
        copy.start()
    inputs[2].wait()
    cells = float(N) ** 3
    wave = (2.0 * math.pi / N) ** 2
    sums = jnp.sum(total[...], axis=1, keepdims=True)
    row = lax.broadcasted_iota(jnp.int32, (8, 1), 0)

    def pick_sum(r):
        return jnp.sum(jnp.where(row == r, sums, 0.0), axis=0, keepdims=True)

    energy_out[...] = pick_sum(0) * (0.5 / cells)
    r3 = lax.broadcasted_iota(jnp.int32, (3, 3), 0)
    c3 = lax.broadcasted_iota(jnp.int32, (3, 3), 1)
    stress = jnp.zeros((3, 3), F32)
    for r, (a, b) in enumerate(((0, 0), (1, 1), (2, 2), (0, 1), (0, 2), (1, 2))):
        here = ((r3 == a) & (c3 == b)) | ((r3 == b) & (c3 == a))
        stress = jnp.where(here, pick_sum(r + 1) * (-0.5 * wave / cells), stress)
    stress_out[...] = stress
    copies = [pltpu.make_async_copy(stress_out, stress_hbm, out_sem.at[8]),
              pltpu.make_async_copy(energy_out, energy_hbm, out_sem.at[9])]
    for copy in copies:
        copy.start()

    inputs[0].wait()
    inputs[1].wait()
    zbh, zbl = bases[0], bases[1]
    for r in range(2):
        block = rows_in[pl.ds(8 + r, N, stride=ROWS), :].T
        out = mm3(split(block), (zbh, zbl)).reshape(4, 2, 16, N)
        for b in range(4):
            for q in range(2):
                u[2 * b + r, 8 + q] = out[b, q]
    for x in range(8):
        block = rows_in[pl.ds(x, N, stride=ROWS), :].T
        u[x, 0:8] = mm3(split(block), (zbh, zbl)).reshape(8, 16, N)
        copies.append(pltpu.make_async_copy(u.at[x], u_out.at[:, x], out_sem.at[x]))
        copies[-1].start()

    for copy in copies:
        copy.wait()


def shards(theta, phi, dphi):
    vmem = pl.BlockSpec(memory_space=pltpu.VMEM)
    free = pl.BlockSpec(memory_space=pl.ANY)
    halves_cube = pltpu.VMEM((Q, 2, HALF, N), F32)
    rows = pltpu.VMEM((N * ROWS, N), F32)
    bases, pick = (jnp.asarray(c) for c in constants())
    received, total = pl.pallas_call(
        kernel,
        out_shape=(
            jax.ShapeDtypeStruct((N * ROWS, N), F32),
            jax.ShapeDtypeStruct((8, N), F32),
        ),
        in_specs=[free] * 5,
        out_specs=(free, vmem),
        scratch_shapes=[
            pltpu.VMEM((Q, 8, 16, N), F32),
            pltpu.VMEM((Q * Q, TABLE), F32),
            pltpu.VMEM((Q * Q, TABLE), F32),
            pltpu.VMEM((5, 2, N, N), BF16),
            pltpu.VMEM((SLOPES, Q * Q), BF16),
            rows, rows, rows, pltpu.VMEM((Q, N, N), F32), halves_cube, halves_cube, halves_cube,
            pltpu.VMEM((Q, 2, 32, N), F32),
            pltpu.VMEM((GROUPS * PAIRS * 8, N), F32),
            pltpu.VMEM((4 * PAIRS + 16, TABLE), BF16),
            pltpu.VMEM((GY, 8, N), F32),
            pltpu.VMEM((GX, 8, N), F32),
            pltpu.VMEM((8, N), F32),
            pltpu.SemaphoreType.DMA((4,)),
            pltpu.SemaphoreType.DMA((2,)),
            pltpu.SemaphoreType.DMA((2,)),
            pltpu.SemaphoreType.DMA((2,)),
            pltpu.SemaphoreType.DMA((2,)),
            pltpu.SemaphoreType.DMA((5,)),
            pltpu.SemaphoreType.DMA((2, 2, GROUPS)),
        ],
        compiler_params=pltpu.CompilerParams(
            collective_id=0, has_side_effects=True, vmem_limit_bytes=56 << 20),
    )(theta, phi.T, dphi.T, bases, pick)
    u, stress, energy = pl.pallas_call(
        finish,
        out_shape=(
            jax.ShapeDtypeStruct((Q, 8, 16, N), F32),
            jax.ShapeDtypeStruct((3, 3), F32),
            jax.ShapeDtypeStruct((1, 1), F32),
        ),
        in_specs=[free] * 3,
        out_specs=(free,) * 3,
        scratch_shapes=[
            rows,
            pltpu.VMEM((8, N), F32),
            pltpu.VMEM((2, N, N), BF16),
            pltpu.VMEM((8, Q, 16, N), F32),
            pltpu.VMEM((3, 3), F32),
            pltpu.VMEM((1, 1), F32),
            pltpu.SemaphoreType.DMA((3,)),
            pltpu.SemaphoreType.DMA((10,)),
        ],
        compiler_params=pltpu.CompilerParams(vmem_limit_bytes=56 << 20),
    )(received, total, bases)
    return u, stress, energy.reshape(())


def solution(mesh):
    return jax.shard_map(
        shards,
        mesh=mesh,
        in_specs=(P(None, "gx", "gy", None), P(), P()),
        out_specs=(P(None, "gx", "gy", None), P(), P()),
        check_vma=False,
    )
```

```python
import functools
import math

import jax
import jax.numpy as jnp
import ml_dtypes
import numpy as np
from jax import lax
from jax.experimental import pallas as pl
from jax.experimental.pallas import tpu as pltpu
from jax.sharding import PartitionSpec as P

MESH = pl.DeviceIdType.MESH
F32 = jnp.float32
BF16 = jnp.bfloat16
N = 128
HALF = 64
Q = 10
GX = 16
REGROUP = 128
FIRST, SECOND = 64, 112
GY = 8
ROWS = 10
VALUES = 104
SLOPES = 56
PAIRS = Q * Q + SLOPES
GROUPS = 9
SPLIT = 4
TABLE = 1024


def real_basis():
    r = np.arange(N)
    rows = [np.full(N, 1.0) / np.sqrt(N)]
    rows += [np.cos(2 * np.pi * k * r / N) * np.sqrt(2.0 / N) for k in range(1, HALF)]
    rows += [np.cos(np.pi * r) / np.sqrt(N)]
    rows += [np.sin(2 * np.pi * k * r / N) * np.sqrt(2.0 / N) for k in range(1, HALF)]
    return np.array(rows)


def halves(array):
    high = array.astype(ml_dtypes.bfloat16)
    low = (array - high.astype(np.float64)).astype(ml_dtypes.bfloat16)
    return np.stack([high, low])


def sym_index(q, p):
    q, p = min(q, p), max(q, p)
    return 100 + q * Q - q * (q - 1) // 2 + (p - q)


def constants():
    basis = real_basis()
    order = np.array([(lane // 2) + HALF * (lane % 2) for lane in range(N)])
    z_basis = basis[order]
    by_source = np.array([(i % GX) * 8 + i // GX for i in range(N)])
    x_basis = basis[:, by_source]
    pick = np.zeros((SLOPES, Q * Q))
    for q in range(Q):
        for p in range(q, Q):
            pick[sym_index(q, p) - Q * Q, q * Q + p] += 0.5
            pick[sym_index(q, p) - Q * Q, p * Q + q] += 0.5
    bases = np.stack([halves(b) for b in (z_basis, x_basis, x_basis.T, basis, basis.T)])
    return bases, pick.astype(ml_dtypes.bfloat16)


def split(value):
    high = value.astype(BF16)
    return high, (value - high.astype(F32)).astype(BF16)


def mm(a, b, dims=(((1,), (0,)), ((), ()))):
    return lax.dot_general(a, b, dims, preferred_element_type=F32)


def mm3(a, b, dims=(((1,), (0,)), ((), ()))):
    (ah, al), (bh, bl) = a, b
    return mm(ah, bh, dims) + (mm(al, bh, dims) + mm(ah, bl, dims))


def lanes_iota(rows):
    return lax.broadcasted_iota(jnp.int32, (rows, N), 1)


def exchange(values, lane_step):
    values = list(values)
    axis = values[0].ndim - 1
    lane = lax.broadcasted_iota(jnp.int32, values[0].shape, axis)
    bit = 1
    while bit < len(values):
        step = bit * lane_step
        low = (lane & step) == 0
        for i in range(len(values)):
            if i & bit:
                continue
            first, second = values[i], values[i | bit]
            values[i] = jnp.where(low, first, pltpu.roll(second, step, axis))
            values[i | bit] = jnp.where(low, pltpu.roll(first, N - step, axis), second)
        bit *= 2
    return values


def exchange_all(values, lane_step):
    count = len(values)
    axis = values[0].ndim - 1
    lane = lax.broadcasted_iota(jnp.int32, values[0].shape, axis)
    turned = [pltpu.roll(value, i * lane_step, axis) if i else value for i, value in enumerate(values)]
    turned = [turned[-i % count] for i in range(count)]
    bit = 1
    while bit < count:
        here = (lane & (bit * lane_step)) != 0
        turned = [jnp.where(here, turned[(i - bit) % count], turned[i]) for i in range(count)]
        bit *= 2
    return [pltpu.roll(value, N - i * lane_step, axis) if i else value for i, value in enumerate(turned)]


def kernel(theta_in, phi_in, dphi_in, bases_in, pick_in, r2, total_out,
           theta, phi, dphi, bases, pick, s1, r1, s2, mid, spec, uspec, grad, partner, ktab, tabs, sums_a, sums_b, part,
           send_sem, recv_sem, own_sem, sib_sem, sum_sem, in_sem, tab_sem):
    inputs = [pltpu.make_async_copy(source, target, in_sem.at[i]) for i, (source, target) in enumerate(
        ((theta_in, theta), (bases_in, bases), (phi_in, phi), (dphi_in, dphi), (pick_in, pick)))]
    for copy in inputs:
        copy.start()
    gx = lax.axis_index("gx")
    gy = lax.axis_index("gy")
    core = lax.rem(gy, 2)
    plane = gx * GY + gy
    place_in_order = gy * GX + gx
    kz_low = plane // 2
    is_znyq = plane == 1
    kz = jnp.where(is_znyq, HALF, kz_low)
    sib = gy + 1 - 2 * core

    barrier = pltpu.get_barrier_semaphore()

    def hello(i, c):
        to = lax.rem(plane + i, N)
        pl.semaphore_signal(barrier, inc=1, device_id=(to // GY, lax.rem(to, GY)), device_id_type=MESH)
        return c

    lax.fori_loop(1, N, hello, 0)

    nt = (((1,), (1,)), ((), ()))
    inputs[0].wait()
    inputs[1].wait()
    zbh, zbl = bases[0, 0], bases[0, 1]
    for x in range(8):
        block = theta[0:8, x].reshape(N, N)
        s1[pl.ds(x, N, stride=ROWS), :] = mm3((zbh, zbl), split(block), nt)
    for r in range(2):
        block = jnp.concatenate([theta[8 + q, 2 * b + r] for b in range(4) for q in range(2)], axis=0)
        s1[pl.ds(8 + r, N, stride=ROWS), :] = mm3((zbh, zbl), split(block), nt)

    for copy in inputs[2:]:
        copy.wait()

    def halves_of(table, first):
        difference = pltpu.roll(table, TABLE - 1, 1) - table
        parts = []
        for value in (table, difference):
            high = value.astype(BF16).astype(F32)
            parts += [high, value - high]
        tabs[first:first + 4 * table.shape[0]] = jnp.concatenate(parts, axis=0).astype(BF16)

    def prepare():
        halves_of(jnp.concatenate([phi[...], jnp.zeros((VALUES - Q * Q, TABLE), F32)], axis=0), 0)
        dphi_h, dphi_l = split(dphi[...])
        halves_of(mm(pick[...], dphi_h) + mm(pick[...], dphi_l), 4 * VALUES)

    lane256 = lax.broadcasted_iota(jnp.int32, (1, 2 * N), 1)
    ky256 = jnp.where(lax.rem(lane256, N) == HALF, HALF, lane256 & (HALF - 1))
    second256 = lane256 // N

    def look_up(step, width):
        row = 2 * step
        first = jnp.where(row > HALF, row - HALF, row)
        near = first * first + kz * kz
        first_tile = 0
        if width < TABLE:
            for t in range(1, (TABLE - width) // N + 1):
                first_tile = first_tile + jnp.minimum(near // math.ceil(t * t * 128.0 * 128.0 * 3 * 4096 / (1023.0 * 1023.0)), 1)
        base = pl.multiple_of(first_tile * N, N)
        kx = row + second256
        kx = jnp.where(kx > HALF, kx - HALF, kx)
        square = kx * kx + ky256 * ky256 + kz * kz
        radial = jnp.sqrt(square.astype(F32)) * ((TABLE - 1) / (HALF * math.sqrt(3.0)))
        lower = jnp.clip(jnp.floor(radial), 0.0, TABLE - 2.0)
        fraction = radial - lower
        index = lower.astype(jnp.int32) - first_tile * N
        points = lax.broadcasted_iota(jnp.int32, (width, 2 * N), 0)
        onehot = jnp.where(points == index, 1.0, 0.0).astype(BF16)
        out = mm(tabs[:, pl.ds(base, width)], onehot)
        for first, count, pair in ((0, VALUES, 0), (4 * VALUES, SLOPES, Q * Q)):
            part = [out[first + i * count:first + (i + 1) * count] for i in range(4)]
            value = (part[0] + part[1]) + fraction * (part[2] + part[3])
            start = (row // 8 * PAIRS + pair) * 8 + row % 8
            ktab[pl.ds(start, count, stride=8), :] = value[:, 0:N]
            ktab[pl.ds(start + 1, count, stride=8), :] = value[:, N:]

    def wide(step, k):
        look_up(step, 768)
        return k

    def narrow(step, k):
        look_up(step, 512)
        return k

    def last(step, k):
        look_up(step, TABLE)
        return k

    def piece(group, slope):
        return ktab.at[pl.ds((group * PAIRS + slope * Q * Q) * 8, (SLOPES if slope else Q * Q) * 8)]

    def share(group, slope):
        mine = piece(group, slope)
        return pltpu.make_async_remote_copy(mine, mine, tab_sem.at[0, slope, group], tab_sem.at[1, slope, group],
                                            device_id=(gx, sib), device_id_type=MESH)

    owned = (range(SPLIT), range(SPLIT, GROUPS))

    def look_group(group):
        for first, until, body in ((0, 15, wide), (15, 32, narrow), (32, 33, last), (33, 36, wide)):
            first, until = max(first, group * 4), min(until, group * 4 + 4)
            if first < until:
                lax.fori_loop(first, until, body, 0)

    shares = plane > 1

    @pl.when(plane <= 1)
    def _():
        prepare()
        for owner in (0, 1):
            @pl.when(core == owner)
            def _(owner=owner):
                for group in owned[1 - owner]:
                    look_group(group)

    pl.semaphore_wait(barrier, N - 1)

    def send1(i, c):
        to = lax.rem(plane + i * 3, N)
        pltpu.make_async_remote_copy(
            s1.at[pl.ds(to * ROWS, ROWS)], r1.at[pl.ds(place_in_order * ROWS, ROWS)], send_sem.at[0], recv_sem.at[0],
            device_id=(to // GY, lax.rem(to, GY)), device_id_type=MESH).start()
        return c

    lax.fori_loop(1, N, send1, 0)
    own1 = pltpu.make_async_copy(
        s1.at[pl.ds(plane * ROWS, ROWS)], r1.at[pl.ds(place_in_order * ROWS, ROWS)], own_sem.at[0])
    own1.start()

    @pl.when(shares)
    def _():
        prepare()

    for owner in (0, 1):
        @pl.when(core == owner)
        def _(owner=owner):
            for group in owned[owner]:
                look_group(group)

                @pl.when(shares)
                def _(group=group):
                    share(group, 0).start()
                    share(group, 1).start()

            @pl.when(shares)
            def _():
                for group in owned[1 - owner]:
                    theirs = piece(group, 0)
                    pltpu.make_async_copy(theirs, theirs, tab_sem.at[1, 0, group]).wait()

    xfh, xfl = bases[1, 0], bases[1, 1]
    all_but_one = pl.ds(0, (N - 1) * ROWS)
    got = r1.at[all_but_one]
    pltpu.make_async_copy(got, got, recv_sem.at[0]).wait()
    own1.wait()
    for g in range(GY):
        block = jnp.concatenate([r1[pl.ds(g * GX * ROWS + x, GX, stride=ROWS), :] for x in range(8)], axis=0)
        mid[g] = mm3((xfh, xfl), split(block))
    for h in range(2):
        ends = [jnp.concatenate([r1[pl.ds((2 * a + h) * GX * ROWS + 8 + r, GX, stride=ROWS), :] for r in range(2)], axis=0)
                for a in range(4)]
        mid[8 + h] = mm3((xfh, xfl), split(jnp.concatenate(exchange(ends, 32), axis=0)))

    def regroup(tile, c):
        place = pl.ds(pl.multiple_of(tile * REGROUP, REGROUP), REGROUP)
        main = exchange_all([mid[i, place] for i in range(8)], 16)
        ends = exchange([mid[i, place] for i in (8, 9)], 16)
        for i, value in enumerate(main + ends):
            mid[i, place] = value
        return c

    lax.fori_loop(0, N // REGROUP, regroup, 0)

    ybh, ybl = bases[4, 0], bases[4, 1]
    for q in range(Q):
        spec[q] = mm3(split(mid[q]), (ybh, ybl)).reshape(2, HALF, N)

    to_sibling = pltpu.make_async_remote_copy(
        spec.at[:, :, pl.ds((1 - core) * 32, 32)], partner, sib_sem.at[0], sib_sem.at[1],
        device_id=(gx, sib), device_id_type=MESH)
    to_sibling.start()

    def contract(tile, energy):
        parity = tile // 8
        place = pl.ds(pl.multiple_of(lax.rem(tile, 8) * 8, 8), 8)
        group = jnp.where(tile == 8, 8, lax.rem(tile, 8))
        s = [spec[q, parity, place] for q in range(Q)]
        for q in range(Q):
            acc = None
            for p in range(Q):
                term = ktab[pl.ds(pl.multiple_of((group * PAIRS + q * Q + p) * 8, 8), 8), :] * s[p]
                acc = term if acc is None else acc + term
            uspec[q, parity, place] = acc
            energy = energy + acc * s[q]
        return energy

    zero = jnp.zeros((8, N), F32)
    energy = lax.fori_loop(0, 16, contract, zero)

    yfh, yfl = bases[3, 0], bases[3, 1]
    for q in range(Q):
        mid[q] = mm3(split(uspec[q].reshape(N, N)), (yfh, yfl))
    lax.fori_loop(0, N // REGROUP, regroup, 0)

    xbh, xbl = bases[2, 0], bases[2, 1]
    for g in range(GY):
        block = mm3((xbh, xbl), split(mid[g]))
        for x in range(8):
            s2[pl.ds(g * GX * ROWS + x, GX, stride=ROWS), :] = block[x * GX:(x + 1) * GX]
    for h in range(2):
        block = mm3((xbh, xbl), split(mid[8 + h]))
        ends = exchange([block[b * 32:(b + 1) * 32] for b in range(4)], 32)
        for a in range(4):
            for r in range(2):
                s2[pl.ds((2 * a + h) * GX * ROWS + 8 + r, GX, stride=ROWS), :] = ends[a][r * GX:(r + 1) * GX]

    def send2(i, c):
        to = lax.rem(plane + i * 3, N)
        to_x, to_y = to // GY, lax.rem(to, GY)
        pltpu.make_async_remote_copy(
            s2.at[pl.ds((to_y * GX + to_x) * ROWS, ROWS)], r2.at[pl.ds(plane * ROWS, ROWS)], send_sem.at[1], recv_sem.at[1],
            device_id=(to_x, to_y), device_id_type=MESH).start()
        return c

    lax.fori_loop(1, FIRST, send2, 0)
    own2 = pltpu.make_async_copy(
        s2.at[pl.ds(place_in_order * ROWS, ROWS)], r2.at[pl.ds(plane * ROWS, ROWS)], own_sem.at[1])
    own2.start()

    for owner in (0, 1):
        @pl.when(shares & (core == owner))
        def _(owner=owner):
            for group in owned[1 - owner]:
                theirs = piece(group, 1)
                pltpu.make_async_copy(theirs, theirs, tab_sem.at[1, 1, group]).wait()
            for group in owned[owner]:
                share(group, 0).wait_send()
                share(group, 1).wait_send()

    lane = lanes_iota(8)
    sub = lax.broadcasted_iota(jnp.int32, (8, N), 0)
    j = lane & (HALF - 1)
    ky_off = j.astype(F32)
    ky_full = jnp.where(lane == HALF, HALF, j).astype(F32)
    sy = lane // HALF
    ynyq = lane == HALF
    top = float(HALF * HALF)
    kz_f = kz.astype(F32)
    kz_off = kz_low.astype(F32)

    def moments(tile, sums):
        parity = tile // 8
        place = pl.ds(pl.multiple_of(lax.rem(tile, 8) * 8, 8), 8)
        group = jnp.where(tile == 8, 8, lax.rem(tile, 8))
        s = [spec[q, parity, place] for q in range(Q)]
        weight = zero
        cross = zero
        for q in range(Q):
            acc = None
            for p in range(Q):
                term = ktab[pl.ds(pl.multiple_of((group * PAIRS + sym_index(q, p)) * 8, 8), 8), :] * s[p]
                acc = term if acc is None else acc + term
            grad[q, parity, place] = acc
            weight = weight + acc * s[q]
            cross = cross + acc * pltpu.roll(spec[q, 1 - parity, place], HALF, 1)
        i = lax.rem(tile, 8) * 8 + sub
        kx_off = i.astype(F32)
        xnyq = (i == 0) & (parity == 1)
        kx_full = jnp.where(xnyq, top, kx_off * kx_off)
        xx, yy, zz, xy, xz, yz = sums
        xx = xx + weight * kx_full
        yy = yy + weight * (ky_full * ky_full)
        zz = zz + weight
        sign = jnp.where(sy == parity, -1.0, 1.0)
        xy = xy + cross * (sign * kx_off * ky_off) + jnp.where(xnyq & ynyq, weight * top, 0.0)
        xz = xz + jnp.where(xnyq & is_znyq, weight * top, 0.0)
        yz = yz + jnp.where(ynyq & is_znyq, weight * top, 0.0)
        return xx, yy, zz, xy, xz, yz

    xx, yy, zz, xy, xz, yz = lax.fori_loop(0, 16, moments, (zero,) * 6)

    to_sibling.wait()

    def mixed(step, sums):
        parity = step // 4
        here = lax.rem(step, 4) * 8
        mine = pl.ds(pl.multiple_of(core * 32 + here, 8), 8)
        theirs = pl.ds(pl.multiple_of(here, 8), 8)
        along_x = zero
        along_y = zero
        for q in range(Q):
            g = grad[q, parity, mine]
            along_x = along_x + g * partner[q, 1 - parity, theirs]
            along_y = along_y + g * pltpu.roll(partner[q, parity, theirs], HALF, 1)
        kx_off = (core * 32 + here + sub).astype(F32)
        xz, yz = sums
        xz = xz + along_x * (jnp.where(parity == core, -2.0, 2.0) * kz_off * kx_off)
        yz = yz + along_y * (jnp.where(sy == core, -2.0, 2.0) * kz_off * ky_off)
        return xz, yz

    xz, yz = lax.fori_loop(0, 8, mixed, (xz, yz))
    zz = zz * (kz_f * kz_f)
    part[...] = zero
    for row, total in enumerate((energy, xx, yy, zz, xy, xz, yz)):
        part[pl.ds(row, 1)] = jnp.sum(total, axis=0, keepdims=True)
    sums_a[gy] = part[...]

    def send_sum_y(i, k):
        to = lax.rem(gy + i, GY)
        pltpu.make_async_remote_copy(part, sums_a.at[gy], send_sem.at[2], sum_sem.at[0],
                                     device_id=(gx, to), device_id_type=MESH).start()
        return k

    lax.fori_loop(1, GY, send_sum_y, 0)
    lax.fori_loop(FIRST, SECOND, send2, 0)

    got = sums_a.at[pl.ds(0, GY - 1)]
    pltpu.make_async_copy(got, got, sum_sem.at[0]).wait()
    total = sums_a[0]
    for i in range(1, GY):
        total = total + sums_a[i]
    sums_b[gx] = total

    def send_sum_x(i, k):
        to = lax.rem(gx + i, GX)
        pltpu.make_async_remote_copy(sums_b.at[gx], sums_b.at[gx], send_sem.at[3], sum_sem.at[1],
                                     device_id=(to, gy), device_id_type=MESH).start()
        return k

    lax.fori_loop(1, GX, send_sum_x, 0)
    lax.fori_loop(SECOND, N, send2, 0)

    got = sums_b.at[pl.ds(0, GX - 1)]
    pltpu.make_async_copy(got, got, sum_sem.at[1]).wait()
    total = sums_b[0]
    for i in range(1, GX):
        total = total + sums_b[i]
    total_out[...] = total

    got = r2.at[all_but_one]
    pltpu.make_async_copy(got, got, recv_sem.at[1]).wait()
    own2.wait()

    for slot, buffer in ((0, s1.at[all_but_one]), (1, s2.at[all_but_one]),
                         (2, sums_a.at[pl.ds(0, GY - 1)]), (3, sums_b.at[pl.ds(0, GX - 1)])):
        pltpu.make_async_copy(buffer, buffer, send_sem.at[slot]).wait()


def finish(received, total_in, bases_in, u_out, stress_hbm, energy_hbm,
           rows_in, total, bases, u, stress_out, energy_out, in_sem, out_sem):
    inputs = [pltpu.make_async_copy(source, target, in_sem.at[i]) for i, (source, target) in enumerate(
        ((received, rows_in), (bases_in.at[0], bases), (total_in, total)))]
    for copy in inputs:
        copy.start()
    inputs[2].wait()
    cells = float(N) ** 3
    wave = (2.0 * math.pi / N) ** 2
    sums = jnp.sum(total[...], axis=1, keepdims=True)
    row = lax.broadcasted_iota(jnp.int32, (8, 1), 0)

    def pick_sum(r):
        return jnp.sum(jnp.where(row == r, sums, 0.0), axis=0, keepdims=True)

    energy_out[...] = pick_sum(0) * (0.5 / cells)
    r3 = lax.broadcasted_iota(jnp.int32, (3, 3), 0)
    c3 = lax.broadcasted_iota(jnp.int32, (3, 3), 1)
    stress = jnp.zeros((3, 3), F32)
    for r, (a, b) in enumerate(((0, 0), (1, 1), (2, 2), (0, 1), (0, 2), (1, 2))):
        here = ((r3 == a) & (c3 == b)) | ((r3 == b) & (c3 == a))
        stress = jnp.where(here, pick_sum(r + 1) * (-0.5 * wave / cells), stress)
    stress_out[...] = stress
    copies = [pltpu.make_async_copy(stress_out, stress_hbm, out_sem.at[8]),
              pltpu.make_async_copy(energy_out, energy_hbm, out_sem.at[9])]
    for copy in copies:
        copy.start()

    inputs[0].wait()
    inputs[1].wait()
    zbh, zbl = bases[0], bases[1]
    for r in range(2):
        block = rows_in[pl.ds(8 + r, N, stride=ROWS), :].T
        out = mm3(split(block), (zbh, zbl)).reshape(4, 2, 16, N)
        for b in range(4):
            for q in range(2):
                u[2 * b + r, 8 + q] = out[b, q]
    for x in range(8):
        block = rows_in[pl.ds(x, N, stride=ROWS), :].T
        u[x, 0:8] = mm3(split(block), (zbh, zbl)).reshape(8, 16, N)
        copies.append(pltpu.make_async_copy(u.at[x], u_out.at[:, x], out_sem.at[x]))
        copies[-1].start()

    for copy in copies:
        copy.wait()


def shards(theta, phi, dphi):
    vmem = pl.BlockSpec(memory_space=pltpu.VMEM)
    free = pl.BlockSpec(memory_space=pl.ANY)
    halves_cube = pltpu.VMEM((Q, 2, HALF, N), F32)
    rows = pltpu.VMEM((N * ROWS, N), F32)
    bases, pick = (jnp.asarray(c) for c in constants())
    received, total = pl.pallas_call(
        kernel,
        out_shape=(
            jax.ShapeDtypeStruct((N * ROWS, N), F32),
            jax.ShapeDtypeStruct((8, N), F32),
        ),
        in_specs=[free] * 5,
        out_specs=(free, vmem),
        scratch_shapes=[
            pltpu.VMEM((Q, 8, 16, N), F32),
            pltpu.VMEM((Q * Q, TABLE), F32),
            pltpu.VMEM((Q * Q, TABLE), F32),
            pltpu.VMEM((5, 2, N, N), BF16),
            pltpu.VMEM((SLOPES, Q * Q), BF16),
            rows, rows, rows, pltpu.VMEM((Q, N, N), F32), halves_cube, halves_cube, halves_cube,
            pltpu.VMEM((Q, 2, 32, N), F32),
            pltpu.VMEM((GROUPS * PAIRS * 8, N), F32),
            pltpu.VMEM((4 * PAIRS + 16, TABLE), BF16),
            pltpu.VMEM((GY, 8, N), F32),
            pltpu.VMEM((GX, 8, N), F32),
            pltpu.VMEM((8, N), F32),
            pltpu.SemaphoreType.DMA((4,)),
            pltpu.SemaphoreType.DMA((2,)),
            pltpu.SemaphoreType.DMA((2,)),
            pltpu.SemaphoreType.DMA((2,)),
            pltpu.SemaphoreType.DMA((2,)),
            pltpu.SemaphoreType.DMA((5,)),
            pltpu.SemaphoreType.DMA((2, 2, GROUPS)),
        ],
        compiler_params=pltpu.CompilerParams(
            collective_id=0, has_side_effects=True, vmem_limit_bytes=56 << 20),
    )(theta, phi.T, dphi.T, bases, pick)
    u, stress, energy = pl.pallas_call(
        finish,
        out_shape=(
            jax.ShapeDtypeStruct((Q, 8, 16, N), F32),
            jax.ShapeDtypeStruct((3, 3), F32),
            jax.ShapeDtypeStruct((1, 1), F32),
        ),
        in_specs=[free] * 3,
        out_specs=(free,) * 3,
        scratch_shapes=[
            rows,
            pltpu.VMEM((8, N), F32),
            pltpu.VMEM((2, N, N), BF16),
            pltpu.VMEM((8, Q, 16, N), F32),
            pltpu.VMEM((3, 3), F32),
            pltpu.VMEM((1, 1), F32),
            pltpu.SemaphoreType.DMA((3,)),
            pltpu.SemaphoreType.DMA((10,)),
        ],
        compiler_params=pltpu.CompilerParams(vmem_limit_bytes=56 << 20),
    )(received, total, bases)
    return u, stress, energy.reshape(())


def solution(mesh):
    return jax.shard_map(
        shards,
        mesh=mesh,
        in_specs=(P(None, "gx", "gy", None), P(), P()),
        out_specs=(P(None, "gx", "gy", None), P(), P()),
        check_vma=False,
    )
```

```python
import functools
import math

import jax
import jax.numpy as jnp
import ml_dtypes
import numpy as np
from jax import lax
from jax.experimental import pallas as pl
from jax.experimental.pallas import tpu as pltpu
from jax.sharding import PartitionSpec as P

MESH = pl.DeviceIdType.MESH
F32 = jnp.float32
BF16 = jnp.bfloat16
N = 128
HALF = 64
Q = 10
GX = 16
REGROUP = 128
FIRST, SECOND = 64, 112
GY = 8
ROWS = 10
VALUES = 104
SLOPES = 56
PAIRS = Q * Q + SLOPES
GROUPS = 9
SPLIT = 4
TABLE = 1024


def real_basis():
    r = np.arange(N)
    rows = [np.full(N, 1.0) / np.sqrt(N)]
    rows += [np.cos(2 * np.pi * k * r / N) * np.sqrt(2.0 / N) for k in range(1, HALF)]
    rows += [np.cos(np.pi * r) / np.sqrt(N)]
    rows += [np.sin(2 * np.pi * k * r / N) * np.sqrt(2.0 / N) for k in range(1, HALF)]
    return np.array(rows)


def halves(array):
    high = array.astype(ml_dtypes.bfloat16)
    low = (array - high.astype(np.float64)).astype(ml_dtypes.bfloat16)
    return np.stack([high, low])


def sym_index(q, p):
    q, p = min(q, p), max(q, p)
    return 100 + q * Q - q * (q - 1) // 2 + (p - q)


def constants():
    basis = real_basis()
    order = np.array([(lane // 2) + HALF * (lane % 2) for lane in range(N)])
    z_basis = basis[order]
    by_source = np.array([(i % GX) * 8 + i // GX for i in range(N)])
    x_basis = basis[:, by_source]
    pick = np.zeros((SLOPES, Q * Q))
    for q in range(Q):
        for p in range(q, Q):
            pick[sym_index(q, p) - Q * Q, q * Q + p] += 0.5
            pick[sym_index(q, p) - Q * Q, p * Q + q] += 0.5
    bases = np.stack([halves(b) for b in (z_basis, x_basis, x_basis.T, basis, basis.T)])
    return bases, pick.astype(ml_dtypes.bfloat16)


def split(value):
    high = value.astype(BF16)
    return high, (value - high.astype(F32)).astype(BF16)


def mm(a, b, dims=(((1,), (0,)), ((), ()))):
    return lax.dot_general(a, b, dims, preferred_element_type=F32)


def mm3(a, b, dims=(((1,), (0,)), ((), ()))):
    (ah, al), (bh, bl) = a, b
    return mm(ah, bh, dims) + (mm(al, bh, dims) + mm(ah, bl, dims))


def lanes_iota(rows):
    return lax.broadcasted_iota(jnp.int32, (rows, N), 1)


def exchange(values, lane_step):
    values = list(values)
    axis = values[0].ndim - 1
    lane = lax.broadcasted_iota(jnp.int32, values[0].shape, axis)
    bit = 1
    while bit < len(values):
        step = bit * lane_step
        low = (lane & step) == 0
        for i in range(len(values)):
            if i & bit:
                continue
            first, second = values[i], values[i | bit]
            values[i] = jnp.where(low, first, pltpu.roll(second, step, axis))
            values[i | bit] = jnp.where(low, pltpu.roll(first, N - step, axis), second)
        bit *= 2
    return values


def exchange_all(values, lane_step):
    count = len(values)
    axis = values[0].ndim - 1
    lane = lax.broadcasted_iota(jnp.int32, values[0].shape, axis)
    turned = [pltpu.roll(value, i * lane_step, axis) if i else value for i, value in enumerate(values)]
    turned = [turned[-i % count] for i in range(count)]
    bit = 1
    while bit < count:
        here = (lane & (bit * lane_step)) != 0
        turned = [jnp.where(here, turned[(i - bit) % count], turned[i]) for i in range(count)]
        bit *= 2
    return [pltpu.roll(value, N - i * lane_step, axis) if i else value for i, value in enumerate(turned)]


def kernel(theta_in, phi_in, dphi_in, bases_in, pick_in, r2, total_out,
           theta, phi, dphi, bases, pick, s1, r1, s2, mid, spec, uspec, grad, partner, ktab, tabs, sums_a, sums_b, part,
           send_sem, recv_sem, own_sem, sib_sem, sum_sem, in_sem, tab_sem, total_here):
    inputs = [pltpu.make_async_copy(source, target, in_sem.at[i]) for i, (source, target) in enumerate(
        ((theta_in, theta), (bases_in, bases), (phi_in, phi), (dphi_in, dphi), (pick_in, pick)))]
    for copy in inputs:
        copy.start()
    gx = lax.axis_index("gx")
    gy = lax.axis_index("gy")
    core = lax.rem(gy, 2)
    plane = gx * GY + gy
    place_in_order = gy * GX + gx
    kz_low = plane // 2
    is_znyq = plane == 1
    kz = jnp.where(is_znyq, HALF, kz_low)
    sib = gy + 1 - 2 * core

    barrier = pltpu.get_barrier_semaphore()

    def hello(i, c):
        to = lax.rem(plane + i, N)
        pl.semaphore_signal(barrier, inc=1, device_id=(to // GY, lax.rem(to, GY)), device_id_type=MESH)
        return c

    lax.fori_loop(1, N, hello, 0)

    nt = (((1,), (1,)), ((), ()))
    inputs[0].wait()
    inputs[1].wait()
    zbh, zbl = bases[0, 0], bases[0, 1]
    for x in range(8):
        block = theta[0:8, x].reshape(N, N)
        s1[pl.ds(x, N, stride=ROWS), :] = mm3((zbh, zbl), split(block), nt)
    for r in range(2):
        block = jnp.concatenate([theta[8 + q, 2 * b + r] for b in range(4) for q in range(2)], axis=0)
        s1[pl.ds(8 + r, N, stride=ROWS), :] = mm3((zbh, zbl), split(block), nt)

    for copy in inputs[2:]:
        copy.wait()

    def halves_of(table, first):
        difference = pltpu.roll(table, TABLE - 1, 1) - table
        parts = []
        for value in (table, difference):
            high = value.astype(BF16).astype(F32)
            parts += [high, value - high]
        tabs[first:first + 4 * table.shape[0]] = jnp.concatenate(parts, axis=0).astype(BF16)

    def prepare():
        halves_of(jnp.concatenate([phi[...], jnp.zeros((VALUES - Q * Q, TABLE), F32)], axis=0), 0)
        dphi_h, dphi_l = split(dphi[...])
        halves_of(mm(pick[...], dphi_h) + mm(pick[...], dphi_l), 4 * VALUES)

    lane256 = lax.broadcasted_iota(jnp.int32, (1, 2 * N), 1)
    ky256 = jnp.where(lax.rem(lane256, N) == HALF, HALF, lane256 & (HALF - 1))
    second256 = lane256 // N

    def look_up(step, width):
        row = 2 * step
        first = jnp.where(row > HALF, row - HALF, row)
        near = first * first + kz * kz
        first_tile = 0
        if width < TABLE:
            for t in range(1, (TABLE - width) // N + 1):
                first_tile = first_tile + jnp.minimum(near // math.ceil(t * t * 128.0 * 128.0 * 3 * 4096 / (1023.0 * 1023.0)), 1)
        base = pl.multiple_of(first_tile * N, N)
        kx = row + second256
        kx = jnp.where(kx > HALF, kx - HALF, kx)
        square = kx * kx + ky256 * ky256 + kz * kz
        radial = jnp.sqrt(square.astype(F32)) * ((TABLE - 1) / (HALF * math.sqrt(3.0)))
        lower = jnp.clip(jnp.floor(radial), 0.0, TABLE - 2.0)
        fraction = radial - lower
        index = lower.astype(jnp.int32) - first_tile * N
        points = lax.broadcasted_iota(jnp.int32, (width, 2 * N), 0)
        onehot = jnp.where(points == index, 1.0, 0.0).astype(BF16)
        out = mm(tabs[:, pl.ds(base, width)], onehot)
        for first, count, pair in ((0, VALUES, 0), (4 * VALUES, SLOPES, Q * Q)):
            part = [out[first + i * count:first + (i + 1) * count] for i in range(4)]
            value = (part[0] + part[1]) + fraction * (part[2] + part[3])
            start = (row // 8 * PAIRS + pair) * 8 + row % 8
            ktab[pl.ds(start, count, stride=8), :] = value[:, 0:N]
            ktab[pl.ds(start + 1, count, stride=8), :] = value[:, N:]

    def wide(step, k):
        look_up(step, 768)
        return k

    def narrow(step, k):
        look_up(step, 512)
        return k

    def last(step, k):
        look_up(step, TABLE)
        return k

    def piece(group, slope):
        return ktab.at[pl.ds((group * PAIRS + slope * Q * Q) * 8, (SLOPES if slope else Q * Q) * 8)]

    def share(group, slope):
        mine = piece(group, slope)
        return pltpu.make_async_remote_copy(mine, mine, tab_sem.at[0, slope, group], tab_sem.at[1, slope, group],
                                            device_id=(gx, sib), device_id_type=MESH)

    owned = (range(SPLIT), range(SPLIT, GROUPS))

    def look_group(group):
        for first, until, body in ((0, 15, wide), (15, 32, narrow), (32, 33, last), (33, 36, wide)):
            first, until = max(first, group * 4), min(until, group * 4 + 4)
            if first < until:
                lax.fori_loop(first, until, body, 0)

    shares = plane > 1

    @pl.when(plane <= 1)
    def _():
        prepare()
        for owner in (0, 1):
            @pl.when(core == owner)
            def _(owner=owner):
                for group in owned[1 - owner]:
                    look_group(group)

    pl.semaphore_wait(barrier, N - 1)

    def send1(i, c):
        to = lax.rem(plane + i * 3, N)
        pltpu.make_async_remote_copy(
            s1.at[pl.ds(to * ROWS, ROWS)], r1.at[pl.ds(place_in_order * ROWS, ROWS)], send_sem.at[0], recv_sem.at[0],
            device_id=(to // GY, lax.rem(to, GY)), device_id_type=MESH).start()
        return c

    lax.fori_loop(1, N, send1, 0)
    own1 = pltpu.make_async_copy(
        s1.at[pl.ds(plane * ROWS, ROWS)], r1.at[pl.ds(place_in_order * ROWS, ROWS)], own_sem.at[0])
    own1.start()

    @pl.when(shares)
    def _():
        prepare()

    for owner in (0, 1):
        @pl.when(core == owner)
        def _(owner=owner):
            for group in owned[owner]:
                look_group(group)

                @pl.when(shares)
                def _(group=group):
                    share(group, 0).start()
                    share(group, 1).start()

            @pl.when(shares)
            def _():
                for group in owned[1 - owner]:
                    theirs = piece(group, 0)
                    pltpu.make_async_copy(theirs, theirs, tab_sem.at[1, 0, group]).wait()

    xfh, xfl = bases[1, 0], bases[1, 1]
    all_but_one = pl.ds(0, (N - 1) * ROWS)
    got = r1.at[all_but_one]
    pltpu.make_async_copy(got, got, recv_sem.at[0]).wait()
    own1.wait()
    for g in range(GY):
        block = jnp.concatenate([r1[pl.ds(g * GX * ROWS + x, GX, stride=ROWS), :] for x in range(8)], axis=0)
        mid[g] = mm3((xfh, xfl), split(block))
    for h in range(2):
        ends = [jnp.concatenate([r1[pl.ds((2 * a + h) * GX * ROWS + 8 + r, GX, stride=ROWS), :] for r in range(2)], axis=0)
                for a in range(4)]
        mid[8 + h] = mm3((xfh, xfl), split(jnp.concatenate(exchange(ends, 32), axis=0)))

    def regroup(tile, c):
        place = pl.ds(pl.multiple_of(tile * REGROUP, REGROUP), REGROUP)
        main = exchange_all([mid[i, place] for i in range(8)], 16)
        ends = exchange([mid[i, place] for i in (8, 9)], 16)
        for i, value in enumerate(main + ends):
            mid[i, place] = value
        return c

    lax.fori_loop(0, N // REGROUP, regroup, 0)

    ybh, ybl = bases[4, 0], bases[4, 1]
    for q in range(Q):
        spec[q] = mm3(split(mid[q]), (ybh, ybl)).reshape(2, HALF, N)

    to_sibling = pltpu.make_async_remote_copy(
        spec.at[:, :, pl.ds((1 - core) * 32, 32)], partner, sib_sem.at[0], sib_sem.at[1],
        device_id=(gx, sib), device_id_type=MESH)
    to_sibling.start()

    def contract(tile, energy):
        parity = tile // 8
        place = pl.ds(pl.multiple_of(lax.rem(tile, 8) * 8, 8), 8)
        group = jnp.where(tile == 8, 8, lax.rem(tile, 8))
        s = [spec[q, parity, place] for q in range(Q)]
        for q in range(Q):
            acc = None
            for p in range(Q):
                term = ktab[pl.ds(pl.multiple_of((group * PAIRS + q * Q + p) * 8, 8), 8), :] * s[p]
                acc = term if acc is None else acc + term
            uspec[q, parity, place] = acc
            energy = energy + acc * s[q]
        return energy

    zero = jnp.zeros((8, N), F32)
    energy = lax.fori_loop(0, 16, contract, zero)

    yfh, yfl = bases[3, 0], bases[3, 1]
    for q in range(Q):
        mid[q] = mm3(split(uspec[q].reshape(N, N)), (yfh, yfl))
    lax.fori_loop(0, N // REGROUP, regroup, 0)

    xbh, xbl = bases[2, 0], bases[2, 1]
    for g in range(GY):
        block = mm3((xbh, xbl), split(mid[g]))
        for x in range(8):
            s2[pl.ds(g * GX * ROWS + x, GX, stride=ROWS), :] = block[x * GX:(x + 1) * GX]
    for h in range(2):
        block = mm3((xbh, xbl), split(mid[8 + h]))
        ends = exchange([block[b * 32:(b + 1) * 32] for b in range(4)], 32)
        for a in range(4):
            for r in range(2):
                s2[pl.ds((2 * a + h) * GX * ROWS + 8 + r, GX, stride=ROWS), :] = ends[a][r * GX:(r + 1) * GX]

    def send2(i, c):
        to = lax.rem(plane + i * 3, N)
        to_x, to_y = to // GY, lax.rem(to, GY)
        pltpu.make_async_remote_copy(
            s2.at[pl.ds((to_y * GX + to_x) * ROWS, ROWS)], r2.at[pl.ds(plane * ROWS, ROWS)], send_sem.at[1], recv_sem.at[1],
            device_id=(to_x, to_y), device_id_type=MESH).start()
        return c

    lax.fori_loop(1, FIRST, send2, 0)
    own2 = pltpu.make_async_copy(
        s2.at[pl.ds(place_in_order * ROWS, ROWS)], r2.at[pl.ds(plane * ROWS, ROWS)], own_sem.at[1])
    own2.start()

    for owner in (0, 1):
        @pl.when(shares & (core == owner))
        def _(owner=owner):
            for group in owned[1 - owner]:
                theirs = piece(group, 1)
                pltpu.make_async_copy(theirs, theirs, tab_sem.at[1, 1, group]).wait()
            for group in owned[owner]:
                share(group, 0).wait_send()
                share(group, 1).wait_send()

    lane = lanes_iota(8)
    sub = lax.broadcasted_iota(jnp.int32, (8, N), 0)
    j = lane & (HALF - 1)
    ky_off = j.astype(F32)
    ky_full = jnp.where(lane == HALF, HALF, j).astype(F32)
    sy = lane // HALF
    ynyq = lane == HALF
    top = float(HALF * HALF)
    kz_f = kz.astype(F32)
    kz_off = kz_low.astype(F32)

    def moments(tile, sums):
        parity = tile // 8
        place = pl.ds(pl.multiple_of(lax.rem(tile, 8) * 8, 8), 8)
        group = jnp.where(tile == 8, 8, lax.rem(tile, 8))
        s = [spec[q, parity, place] for q in range(Q)]
        weight = zero
        cross = zero
        for q in range(Q):
            acc = None
            for p in range(Q):
                term = ktab[pl.ds(pl.multiple_of((group * PAIRS + sym_index(q, p)) * 8, 8), 8), :] * s[p]
                acc = term if acc is None else acc + term
            grad[q, parity, place] = acc
            weight = weight + acc * s[q]
            cross = cross + acc * pltpu.roll(spec[q, 1 - parity, place], HALF, 1)
        i = lax.rem(tile, 8) * 8 + sub
        kx_off = i.astype(F32)
        xnyq = (i == 0) & (parity == 1)
        kx_full = jnp.where(xnyq, top, kx_off * kx_off)
        xx, yy, zz, xy, xz, yz = sums
        xx = xx + weight * kx_full
        yy = yy + weight * (ky_full * ky_full)
        zz = zz + weight
        sign = jnp.where(sy == parity, -1.0, 1.0)
        xy = xy + cross * (sign * kx_off * ky_off) + jnp.where(xnyq & ynyq, weight * top, 0.0)
        xz = xz + jnp.where(xnyq & is_znyq, weight * top, 0.0)
        yz = yz + jnp.where(ynyq & is_znyq, weight * top, 0.0)
        return xx, yy, zz, xy, xz, yz

    xx, yy, zz, xy, xz, yz = lax.fori_loop(0, 16, moments, (zero,) * 6)

    to_sibling.wait()

    def mixed(step, sums):
        parity = step // 4
        here = lax.rem(step, 4) * 8
        mine = pl.ds(pl.multiple_of(core * 32 + here, 8), 8)
        theirs = pl.ds(pl.multiple_of(here, 8), 8)
        along_x = zero
        along_y = zero
        for q in range(Q):
            g = grad[q, parity, mine]
            along_x = along_x + g * partner[q, 1 - parity, theirs]
            along_y = along_y + g * pltpu.roll(partner[q, parity, theirs], HALF, 1)
        kx_off = (core * 32 + here + sub).astype(F32)
        xz, yz = sums
        xz = xz + along_x * (jnp.where(parity == core, -2.0, 2.0) * kz_off * kx_off)
        yz = yz + along_y * (jnp.where(sy == core, -2.0, 2.0) * kz_off * ky_off)
        return xz, yz

    xz, yz = lax.fori_loop(0, 8, mixed, (xz, yz))
    zz = zz * (kz_f * kz_f)
    part[...] = zero
    for row, total in enumerate((energy, xx, yy, zz, xy, xz, yz)):
        part[pl.ds(row, 1)] = jnp.sum(total, axis=0, keepdims=True)
    sums_a[gy] = part[...]

    def send_sum_y(i, k):
        to = lax.rem(gy + i, GY)
        pltpu.make_async_remote_copy(part, sums_a.at[gy], send_sem.at[2], sum_sem.at[0],
                                     device_id=(gx, to), device_id_type=MESH).start()
        return k

    lax.fori_loop(1, GY, send_sum_y, 0)
    lax.fori_loop(FIRST, SECOND, send2, 0)

    got = sums_a.at[pl.ds(0, GY - 1)]
    pltpu.make_async_copy(got, got, sum_sem.at[0]).wait()
    total = sums_a[0]
    for i in range(1, GY):
        total = total + sums_a[i]
    sums_b[gx] = total

    def send_sum_x(i, k):
        to = lax.rem(gx + i, GX)
        pltpu.make_async_remote_copy(sums_b.at[gx], sums_b.at[gx], send_sem.at[3], sum_sem.at[1],
                                     device_id=(to, gy), device_id_type=MESH).start()
        return k

    lax.fori_loop(1, GX, send_sum_x, 0)
    lax.fori_loop(SECOND, N, send2, 0)

    got = sums_b.at[pl.ds(0, GX - 1)]
    pltpu.make_async_copy(got, got, sum_sem.at[1]).wait()
    total = sums_b[0]
    for i in range(1, GX):
        total = total + sums_b[i]
    total_here[...] = total
    total_copy = pltpu.make_async_copy(total_here, total_out, in_sem.at[4])
    total_copy.start()

    got = r2.at[all_but_one]
    pltpu.make_async_copy(got, got, recv_sem.at[1]).wait()
    own2.wait()
    total_copy.wait()

    for slot, buffer in ((0, s1.at[all_but_one]), (1, s2.at[all_but_one]),
                         (2, sums_a.at[pl.ds(0, GY - 1)]), (3, sums_b.at[pl.ds(0, GX - 1)])):
        pltpu.make_async_copy(buffer, buffer, send_sem.at[slot]).wait()


def finish(received, total_in, bases_in, u_out, stress_hbm, energy_hbm,
           rows_in, total, bases, u, stress_out, energy_out, in_sem, out_sem):
    inputs = [pltpu.make_async_copy(source, target, in_sem.at[i]) for i, (source, target) in enumerate(
        ((received, rows_in), (bases_in.at[0], bases), (total_in, total)))]
    for copy in inputs:
        copy.start()
    inputs[2].wait()
    cells = float(N) ** 3
    wave = (2.0 * math.pi / N) ** 2
    sums = jnp.sum(total[...], axis=1, keepdims=True)
    row = lax.broadcasted_iota(jnp.int32, (8, 1), 0)

    def pick_sum(r):
        return jnp.sum(jnp.where(row == r, sums, 0.0), axis=0, keepdims=True)

    energy_out[...] = pick_sum(0) * (0.5 / cells)
    r3 = lax.broadcasted_iota(jnp.int32, (3, 3), 0)
    c3 = lax.broadcasted_iota(jnp.int32, (3, 3), 1)
    stress = jnp.zeros((3, 3), F32)
    for r, (a, b) in enumerate(((0, 0), (1, 1), (2, 2), (0, 1), (0, 2), (1, 2))):
        here = ((r3 == a) & (c3 == b)) | ((r3 == b) & (c3 == a))
        stress = jnp.where(here, pick_sum(r + 1) * (-0.5 * wave / cells), stress)
    stress_out[...] = stress
    copies = [pltpu.make_async_copy(stress_out, stress_hbm, out_sem.at[8]),
              pltpu.make_async_copy(energy_out, energy_hbm, out_sem.at[9])]
    for copy in copies:
        copy.start()

    inputs[0].wait()
    inputs[1].wait()
    zbh, zbl = bases[0], bases[1]
    for r in range(2):
        block = rows_in[pl.ds(8 + r, N, stride=ROWS), :].T
        out = mm3(split(block), (zbh, zbl)).reshape(4, 2, 16, N)
        for b in range(4):
            for q in range(2):
                u[2 * b + r, 8 + q] = out[b, q]
    for x in range(8):
        block = rows_in[pl.ds(x, N, stride=ROWS), :].T
        u[x, 0:8] = mm3(split(block), (zbh, zbl)).reshape(8, 16, N)
        copies.append(pltpu.make_async_copy(u.at[x], u_out.at[:, x], out_sem.at[x]))
        copies[-1].start()

    for copy in copies:
        copy.wait()


def shards(theta, phi, dphi):
    vmem = pl.BlockSpec(memory_space=pltpu.VMEM)
    free = pl.BlockSpec(memory_space=pl.ANY)
    halves_cube = pltpu.VMEM((Q, 2, HALF, N), F32)
    rows = pltpu.VMEM((N * ROWS, N), F32)
    bases, pick = (jnp.asarray(c) for c in constants())
    received, total = pl.pallas_call(
        kernel,
        out_shape=(
            jax.ShapeDtypeStruct((N * ROWS, N), F32),
            jax.ShapeDtypeStruct((8, N), F32),
        ),
        in_specs=[free] * 5,
        out_specs=(free, free),
        scratch_shapes=[
            pltpu.VMEM((Q, 8, 16, N), F32),
            pltpu.VMEM((Q * Q, TABLE), F32),
            pltpu.VMEM((Q * Q, TABLE), F32),
            pltpu.VMEM((5, 2, N, N), BF16),
            pltpu.VMEM((SLOPES, Q * Q), BF16),
            rows, rows, rows, pltpu.VMEM((Q, N, N), F32), halves_cube, halves_cube, halves_cube,
            pltpu.VMEM((Q, 2, 32, N), F32),
            pltpu.VMEM((GROUPS * PAIRS * 8, N), F32),
            pltpu.VMEM((4 * PAIRS + 16, TABLE), BF16),
            pltpu.VMEM((GY, 8, N), F32),
            pltpu.VMEM((GX, 8, N), F32),
            pltpu.VMEM((8, N), F32),
            pltpu.SemaphoreType.DMA((4,)),
            pltpu.SemaphoreType.DMA((2,)),
            pltpu.SemaphoreType.DMA((2,)),
            pltpu.SemaphoreType.DMA((2,)),
            pltpu.SemaphoreType.DMA((2,)),
            pltpu.SemaphoreType.DMA((5,)),
            pltpu.SemaphoreType.DMA((2, 2, GROUPS)),
            pltpu.VMEM((8, N), F32),
        ],
        compiler_params=pltpu.CompilerParams(
            collective_id=0, has_side_effects=True, vmem_limit_bytes=56 << 20),
    )(theta, phi.T, dphi.T, bases, pick)
    u, stress, energy = pl.pallas_call(
        finish,
        out_shape=(
            jax.ShapeDtypeStruct((Q, 8, 16, N), F32),
            jax.ShapeDtypeStruct((3, 3), F32),
            jax.ShapeDtypeStruct((1, 1), F32),
        ),
        in_specs=[free] * 3,
        out_specs=(free,) * 3,
        scratch_shapes=[
            rows,
            pltpu.VMEM((8, N), F32),
            pltpu.VMEM((2, N, N), BF16),
            pltpu.VMEM((8, Q, 16, N), F32),
            pltpu.VMEM((3, 3), F32),
            pltpu.VMEM((1, 1), F32),
            pltpu.SemaphoreType.DMA((3,)),
            pltpu.SemaphoreType.DMA((10,)),
        ],
        compiler_params=pltpu.CompilerParams(vmem_limit_bytes=56 << 20),
    )(received, total, bases)
    return u, stress, energy.reshape(())


def solution(mesh):
    return jax.shard_map(
        shards,
        mesh=mesh,
        in_specs=(P(None, "gx", "gy", None), P(), P()),
        out_specs=(P(None, "gx", "gy", None), P(), P()),
        check_vma=False,
    )
```
